256 devices in a mesh: seq: 32 (over z, x), dp: 8 (over y, core).
Axes of the slice: x: 4, y: 4, z: 8, core: 2. Of those that a mesh axis runs over, the one named last changes fastest.
Arguments:
- queries: bfloat16 [8, 4096, 1024], P('dp', 'seq'), may hold values from -40 to 40
- keys: bfloat16 [8, 4096, 1024], P('dp', 'seq'), may hold values from -4 to 4
- values: bfloat16 [8, 4096, 1024], P('dp', 'seq'), may hold values from -6 to 6
- d_out: bfloat16 [8, 4096, 1024], P('dp', 'seq'), may hold values from -6 to 6
- w_out: bfloat16 [1024, 1024], replicated, may hold values from -0.1875 to 0.1875
Outputs:
- d_queries: bfloat16 [8, 4096, 1024], P('dp', 'seq')
- d_keys: bfloat16 [8, 4096, 1024], P('dp', 'seq')
- d_values: bfloat16 [8, 4096, 1024], P('dp', 'seq')
- grad_w_out: float32 [1024, 1024], P('seq', 'dp')
The draws below stay inside these ranges and needn't reach their ends.
All inputs are finite; a program needn't handle non-finite values.
Results may differ from the reference program's by a relative error of at most 0.017.
Values may be sent and summed in bfloat16 or wider, within the bound.
A program may use at most 128 MiB of HBM per device.

```python
import jax
import jax.numpy as jnp
from jax import lax

HEADS = 16
HEAD_DIM = 64
WIDTH = 1024
BLOCK = 16
LEVELS = 5
SEQ_DEV = 128
TOKENS = 4096
SEQS = 8
N_SEQ = 32


def draw_queries(key, part):
    key = jax.random.fold_in(key, 3)
    return jnp.clip(jax.random.normal(key, (SEQS, TOKENS, WIDTH), jnp.float32), -4.0, 4.0).astype(jnp.bfloat16)


def draw_keys(key, part):
    key = jax.random.fold_in(key, 5)
    return jnp.clip(jax.random.normal(key, (SEQS, TOKENS, WIDTH), jnp.float32), -4.0, 4.0).astype(jnp.bfloat16)


def strengthened(drawn, rng, source, target, shards_of, factor):
    def block_of(position):
        return (jnp.arange(drawn.shape[position]) // (drawn.shape[position] // shards_of)).reshape((-1,) + (1,) * (drawn.ndim - 1 - position))

    near = jax.random.permutation(rng, shards_of)[block_of(target)]
    far = (block_of(target) + shards_of // 2) % shards_of
    return jnp.where((block_of(source) == near) | (block_of(source) == far), factor * drawn, drawn)


def steps_of(key, shape, pieces, smallest, largest):
    factor_of, own = 1.0, jax.random.fold_in(key, 6)
    for position, shards_of in pieces:
        draws = jnp.exp(jax.random.uniform(jax.random.fold_in(own, position), (shards_of,), jnp.float32, smallest / len(pieces), largest / len(pieces)))
        factor_of = factor_of * jnp.repeat(draws, shape[position] // shards_of).reshape([-1 if axis == position else 1 for axis in range(len(shape))])
    return factor_of


def normal_values(rng, dims, spread, reach, cuts=(), kind=jnp.bfloat16):
    loudness = steps_of(rng, dims, cuts, -0.22, 0.18) if cuts else 1.0
    result = jax.random.normal(rng, dims, jnp.float32) * spread * loudness
    return jnp.minimum(jnp.maximum(result, -reach), reach).astype(kind)


def bell_draw_with(key, dims, width, most, shards, heavy, held_as=jnp.bfloat16):
    values = width * jax.random.normal(key, dims, jnp.float32)
    if shards:
        values = values * steps_of(key, dims, shards, -0.22, 0.18)
    return jnp.clip(strengthened(values, jax.random.fold_in(key, 3), *heavy), -most, most).astype(held_as)


def setup_inputs(seed: int = 0) -> dict:
    arg_keys = jax.random.split(jax.random.key(seed), 6)
    queries = draw_queries(jax.random.fold_in(arg_keys[5], 71), 0)
    keys = draw_keys(jax.random.fold_in(arg_keys[5], 71), 0)
    values = normal_values(arg_keys[2], (SEQS, TOKENS, WIDTH), 1.0, 6.0, ((0, 8), (1, 32)))
    d_out = bell_draw_with(arg_keys[3], (SEQS, TOKENS, WIDTH), 1.0, 6.0, ((0, 8), (1, 32)), (0, 2, 8, 2.0))
    w_out = normal_values(arg_keys[4], (WIDTH, WIDTH), WIDTH ** -0.5, 0.1875)
    return {"queries": queries, "keys": keys, "values": values, "d_out": d_out, "w_out": w_out}


def product_exact(formula, first_op, second_op):
    return jnp.einsum(formula, first_op.astype(jnp.float32), second_op.astype(jnp.float32))


def pooled(fields, level_id):
    if level_id == 0:
        return fields
    span_tokens = 2 ** level_id
    summed = jnp.sum(fields.astype(jnp.float32).reshape(fields.shape[0] // span_tokens, span_tokens, fields.shape[1]), axis=1)
    return (summed * (span_tokens ** -0.5)).astype(jnp.bfloat16)


def level_plan(level_id, row_count):
    amount = row_count // 2 ** level_id
    span_tokens = BLOCK * 2 ** level_id
    if span_tokens <= row_count:
        return amount, True, amount // BLOCK, 1
    return amount, False, 1, span_tokens // row_count


def make_windows(extended, level_id, group_count, blocked):
    if not blocked:
        return extended.reshape((1,) + extended.shape)
    tail_shape = extended.shape[1:]
    blocks = extended.reshape((group_count + 2, extended.shape[0] // (group_count + 2)) + tail_shape)
    if level_id == 0:
        parts = [blocks[:-2], blocks[1:-1], blocks[2:]]
    else:
        parts = [blocks[:-2], blocks[2:]]
    return jnp.concatenate(parts, axis=1)


def unfold_windows(gradient, level_id, group_count, blocked):
    if not blocked:
        return gradient.reshape(gradient.shape[1:])
    placements = [0, 1, 2] if level_id == 0 else [0, 2]
    block_len = gradient.shape[1] // len(placements)
    tail_shape = gradient.shape[2:]
    tail_pads = [(0, 0)] * (len(tail_shape) + 1)
    summed = jnp.zeros((group_count + 2, block_len) + tail_shape, gradient.dtype)
    for number, placement in enumerate(placements):
        segment = gradient[:, number * block_len:(number + 1) * block_len]
        summed = summed + jnp.pad(segment, [(placement, 2 - placement)] + tail_pads)
    return summed.reshape(((group_count + 2) * block_len,) + tail_shape)


def block_attention(query_heads, grad_heads, wins_k, wins_v, valids, product):
    row_count, head_count, head_dim = query_heads.shape
    key_scale = head_dim ** -0.5
    scores = []
    for win_k, valid_mask in zip(wins_k, valids):
        group_count = win_k.shape[0]
        grouped = query_heads.reshape(group_count, row_count // group_count, head_count, head_dim)
        part_scores = product("gqhe,gkhe->gqhk", grouped, win_k) * key_scale
        part_scores = jnp.where(valid_mask[:, None, None, :], part_scores, -jnp.inf)
        scores.append(part_scores.reshape(row_count, head_count, win_k.shape[1]))
    scores = jnp.concatenate(scores, axis=2)
    row_top = jnp.max(scores, axis=2, keepdims=True)
    exponent = jnp.exp(scores - row_top)
    weights = exponent / jnp.sum(exponent, axis=2, keepdims=True)
    weights_half = weights.astype(jnp.bfloat16)
    mixture = jnp.zeros((row_count, head_count, head_dim), jnp.float32)
    weight_parts = []
    offset = 0
    for win_v in wins_v:
        group_count, key_count = win_v.shape[0], win_v.shape[1]
        weight_part = weights_half[:, :, offset:offset + key_count].reshape(group_count, row_count // group_count, head_count, key_count)
        mixture = mixture + product("gqhk,gkhe->gqhe", weight_part, win_v).reshape(row_count, head_count, head_dim)
        weight_parts.append(weight_part)
        offset += key_count
    attended = mixture.astype(jnp.bfloat16)
    row_delta = jnp.sum(grad_heads.astype(jnp.float32) * attended.astype(jnp.float32), axis=2, keepdims=True)
    d_prob = []
    for win_v in wins_v:
        group_count = win_v.shape[0]
        grouped_grad = grad_heads.reshape(group_count, row_count // group_count, head_count, head_dim)
        d_prob.append(product("gqhe,gkhe->gqhk", grouped_grad, win_v).reshape(row_count, head_count, win_v.shape[1]))
    d_prob = jnp.concatenate(d_prob, axis=2)
    d_score = (weights * (d_prob - row_delta)).astype(jnp.bfloat16)
    d_query = jnp.zeros((row_count, head_count, head_dim), jnp.float32)
    grads_k = []
    grads_v = []
    offset = 0
    for win_k, win_v, weight_part in zip(wins_k, wins_v, weight_parts):
        group_count, key_count = win_k.shape[0], win_k.shape[1]
        score_part = d_score[:, :, offset:offset + key_count].reshape(group_count, row_count // group_count, head_count, key_count)
        grouped = query_heads.reshape(group_count, row_count // group_count, head_count, head_dim)
        grouped_grad = grad_heads.reshape(group_count, row_count // group_count, head_count, head_dim)
        d_query = d_query + product("gqhk,gkhe->gqhe", score_part, win_k).reshape(row_count, head_count, head_dim)
        grads_k.append(product("gqhk,gqhe->gkhe", score_part, grouped) * key_scale)
        grads_v.append(product("gqhk,gqhe->gkhe", weight_part, grouped_grad))
        offset += key_count
    return attended, (d_query * key_scale).astype(jnp.bfloat16), grads_k, grads_v


def one_sequence(inputs):
    query_rows, key_rows, value_rows, grad_rows = inputs
    level_plans = [level_plan(level_id, SEQ_DEV) for level_id in range(LEVELS)]
    padded_k = []
    padded_v = []
    for level_id in range(LEVELS):
        coarse_k = pooled(key_rows, level_id).reshape(-1, HEADS, HEAD_DIM)
        coarse_v = pooled(value_rows, level_id).reshape(-1, HEADS, HEAD_DIM)
        padded_k.append(jnp.pad(coarse_k, ((BLOCK, 2 * BLOCK), (0, 0), (0, 0))))
        padded_v.append(jnp.pad(coarse_v, ((BLOCK, 2 * BLOCK), (0, 0), (0, 0))))
    heads_q = query_rows.reshape(TOKENS, HEADS, HEAD_DIM)
    heads_g = grad_rows.reshape(TOKENS, HEADS, HEAD_DIM)

    def block_step(carried, block_index):
        sums_k, sums_v = carried
        block_q = lax.dynamic_slice_in_dim(heads_q, block_index * SEQ_DEV, SEQ_DEV, 0)
        block_g = lax.dynamic_slice_in_dim(heads_g, block_index * SEQ_DEV, SEQ_DEV, 0)
        wins_k, wins_v, valids, slices = [], [], [], []
        for level_id in range(LEVELS):
            amount, blocked, group_count, group_size = level_plans[level_id]
            if blocked:
                level_slices = [(block_index * amount, amount + 2 * BLOCK)]
                positions = block_index * amount - BLOCK + jnp.arange(amount + 2 * BLOCK, dtype=jnp.int32)
            else:
                corner = block_index // group_size
                level_slices = [(corner * BLOCK, BLOCK), ((corner + 2) * BLOCK, BLOCK)]
                within = jnp.arange(BLOCK, dtype=jnp.int32)
                positions = jnp.concatenate([(corner - 1) * BLOCK + within, (corner + 1) * BLOCK + within])
            valid_mask = (positions >= 0) & (positions < N_SEQ * amount)
            ext_k = jnp.concatenate([lax.dynamic_slice_in_dim(padded_k[level_id], begin, length, 0) for begin, length in level_slices], axis=0)
            ext_v = jnp.concatenate([lax.dynamic_slice_in_dim(padded_v[level_id], begin, length, 0) for begin, length in level_slices], axis=0)
            wins_k.append(make_windows(ext_k, level_id, group_count, blocked))
            wins_v.append(make_windows(ext_v, level_id, group_count, blocked))
            valids.append(make_windows(valid_mask, level_id, group_count, blocked))
            slices.append(level_slices)
        attended, d_query, grads_k, grads_v = block_attention(block_q, block_g, wins_k, wins_v, valids, product_exact)
        new_k, new_v = [], []
        for level_id in range(LEVELS):
            amount, blocked, group_count, group_size = level_plans[level_id]
            back_k = unfold_windows(grads_k[level_id], level_id, group_count, blocked)
            back_v = unfold_windows(grads_v[level_id], level_id, group_count, blocked)
            target_k, target_v = sums_k[level_id], sums_v[level_id]
            offset = 0
            for begin, length in slices[level_id]:
                piece_k = back_k[offset:offset + length]
                piece_v = back_v[offset:offset + length]
                target_k = lax.dynamic_update_slice_in_dim(target_k, lax.dynamic_slice_in_dim(target_k, begin, length, 0) + piece_k, begin, 0)
                target_v = lax.dynamic_update_slice_in_dim(target_v, lax.dynamic_slice_in_dim(target_v, begin, length, 0) + piece_v, begin, 0)
                offset += length
            new_k.append(target_k)
            new_v.append(target_v)
        return (new_k, new_v), (attended, d_query)

    start_k = [jnp.zeros(padded.shape, jnp.float32) for padded in padded_k]
    start_v = [jnp.zeros(padded.shape, jnp.float32) for padded in padded_v]
    (sums_k, sums_v), (attended, d_query) = lax.scan(block_step, (start_k, start_v), jnp.arange(N_SEQ, dtype=jnp.int32))
    d_key = jnp.zeros((TOKENS, WIDTH), jnp.float32)
    d_value = jnp.zeros((TOKENS, WIDTH), jnp.float32)
    for level_id in range(LEVELS):
        span_tokens = 2 ** level_id
        amount = TOKENS // span_tokens
        level_k = sums_k[level_id][BLOCK:BLOCK + amount].reshape(amount, WIDTH)
        level_v = sums_v[level_id][BLOCK:BLOCK + amount].reshape(amount, WIDTH)
        d_key = d_key + jnp.broadcast_to(level_k[:, None, :], (amount, span_tokens, WIDTH)).reshape(TOKENS, WIDTH) * (span_tokens ** -0.5)
        d_value = d_value + jnp.broadcast_to(level_v[:, None, :], (amount, span_tokens, WIDTH)).reshape(TOKENS, WIDTH) * (span_tokens ** -0.5)
    return (attended.reshape(TOKENS, WIDTH), d_query.reshape(TOKENS, WIDTH), d_key.astype(jnp.bfloat16), d_value.astype(jnp.bfloat16))


def reference(queries, keys, values, d_out, w_out):
    grad_heads = jnp.dot(d_out.reshape(-1, WIDTH), w_out.T, preferred_element_type=jnp.float32).astype(jnp.bfloat16)
    grad_heads = grad_heads.reshape(SEQS, TOKENS, WIDTH)
    attended, d_queries, d_keys, d_values = lax.map(one_sequence, (queries, keys, values, grad_heads))
    factor = (SEQS * TOKENS) ** -0.5
    grad_w_out = jnp.dot(attended.reshape(-1, WIDTH).T, d_out.reshape(-1, WIDTH), preferred_element_type=jnp.float32) * factor
    return d_queries, d_keys, d_values, grad_w_out
```

```python
import jax
import jax.numpy as jnp
from jax import lax
from jax.experimental import pallas as pl
from jax.experimental.pallas import tpu as pltpu
from jax.sharding import PartitionSpec as P

ROWS = 128
WIDTH = 1024
PAIR = 128
PAIRS = 8
KEYS = 384
N_SEQ = 32
X, Z = 4, 8
FACTOR = 32768 ** (-0.5)
MESH = pl.DeviceIdType.MESH
F32 = jnp.float32
BF16 = jnp.bfloat16

OWN1, OWN2, LEFT, RIGHT, LEFT4, RIGHT4 = 128, 192, 224, 288, 352, 368


def dot_nt(a, b):
    return lax.dot_general(a, b, (((1,), (1,)), ((), ())), preferred_element_type=F32)


def dot_tn(a, b):
    return lax.dot_general(a, b, (((0,), (0,)), ((), ())), preferred_element_type=F32)


def dot_nn(a, b):
    return lax.dot_general(a, b, (((1,), (0,)), ((), ())), preferred_element_type=F32)


def two_heads(block, scale):
    lane = lax.broadcasted_iota(jnp.int32, (1, PAIR), 1)
    first = jnp.where(lane < 64, scale, 0.0).astype(BF16)
    second = jnp.where(lane < 64, 0.0, scale).astype(BF16)
    return jnp.concatenate([block * first, block * second], axis=0)


def one_of_two(both):
    row = lax.broadcasted_iota(jnp.int32, (PAIR, ROWS), 0)
    return jnp.where(row < 64, both[:, :ROWS], both[:, ROWS:])


def pool_matrix():
    row = lax.broadcasted_iota(jnp.int32, (ROWS, ROWS), 0)
    token = lax.broadcasted_iota(jnp.int32, (ROWS, ROWS), 1)
    level = jnp.where(row < 64, 1, jnp.where(row < 96, 2, jnp.where(row < 112, 3, 4)))
    base = jnp.where(row < 64, 0, jnp.where(row < 96, 64, jnp.where(row < 112, 96, 112)))
    matrix = jnp.where(lax.shift_right_logical(token, level) == row - base, 1.0, 0.0).astype(BF16)
    row = lax.broadcasted_iota(jnp.int32, (ROWS, 1), 0)
    scale = jnp.where(
        row < 64, 2.0 ** (-0.5), jnp.where(row < 96, 0.5, jnp.where(row < 112, 2.0 ** (-1.5), 0.25))
    ).astype(F32)
    return matrix, scale


def spread_matrix():
    token = lax.broadcasted_iota(jnp.int32, (ROWS, 256), 0)
    row = lax.broadcasted_iota(jnp.int32, (ROWS, 256), 1)
    in_rim = lax.rem(row - 96, 64)
    rim_level = in_rim // 16
    within = lax.rem(in_rim, 16)
    rim_last = jnp.where(rim_level == 0, 112, jnp.where(rim_level == 1, 48, jnp.where(rim_level == 2, 16, 0)))
    level = jnp.where(row < 64, 1, jnp.where(row < 96, 2, jnp.where(row < 224, rim_level, 4)))
    target = jnp.where(
        row < 64,
        row,
        jnp.where(
            row < 96,
            row - 64,
            jnp.where(row < 160, rim_last + within, jnp.where(row < 224, within, lax.rem(row - 224, 8))),
        ),
    )
    return jnp.where(lax.shift_right_logical(token, level) == target, 1.0, 0.0).astype(BF16)


def fill_bias(bias, device):
    token = lax.rem(lax.broadcasted_iota(jnp.int32, (16, 2 * ROWS), 1), ROWS)
    not_first = device > 0
    not_last = device < N_SEQ - 1

    def put(row, valid):
        bias[row : row + 16, :] = jnp.where(valid, 0.0, -1e30).astype(F32)

    for block in range(8):
        near = token // 16 - block
        put(16 * block, (near >= -1) & (near <= 1))
    for block in range(4):
        near = token // 32 - block
        put(OWN1 + 16 * block, (near == -1) | (near == 1))
    for block in range(2):
        put(OWN2 + 16 * block, token // 64 != block)
    for level in range(4):
        span = 16 * 2**level
        put(LEFT + 16 * level, (token < span) & not_first)
        put(RIGHT + 16 * level, (token >= ROWS - span) & not_last)
    always = token >= 0
    put(LEFT4, always & (device >= 2))
    put(RIGHT4, always & (device < N_SEQ - 2))


def kernel(
    q_hbm, k_hbm, v_hbm, d_hbm, w_hbm,
    dq_ref, dk_ref, dv_ref, gw_ref,
    q, d, w, g, kv, bias, spread,
    rim, four, four_in,
    weights, own, back, back_rim, back_four, back_four_in,
    pairs_a, pairs_d, kept, kept2, y1_out, y1_in, y2_out, y2_in, z_out, z_in, x_out, x_in,
    in_sem, rim_s, rim_r, four_s, four_r, d2_s, d2_r, a_s, a_r, y1_s, y1_r, y2_s, y2_r,
    z_s, z_r, x_s, x_r, back_s, back_r, bfour_s, bfour_r,
):
    seq = lax.axis_index("seq")
    dp = lax.axis_index("dp")
    z, x = lax.div(seq, X), lax.rem(seq, X)
    y, core = lax.div(dp, 2), lax.rem(dp, 2)
    ya = y + 1 - 2 * lax.rem(y, 2)
    yb = 3 - y
    yo = 3 - ya
    pair_of = lax.div(seq, 2)
    parity = lax.rem(seq, 2)

    def at(seq_to, dp_to):
        return {"seq": seq_to, "dp": dp_to}

    right = at(lax.rem(seq + 1, N_SEQ), dp)
    left = at(lax.rem(seq + N_SEQ - 1, N_SEQ), dp)
    twin = at(seq, 2 * y + 1 - core)
    at_ya = at(seq, 2 * ya + core)
    at_yb = at(seq, 2 * yb + core)
    fours = []
    for side in (0, 1):
        block = lax.rem(pair_of + (N_SEQ // 2 - 1 if side == 0 else 1), N_SEQ // 2)
        for part in (0, 1):
            fours.append(at(2 * block + part, dp))

    def at_z(step):
        return at(lax.rem(z + 1 + step, Z) * X + x, dp)

    def at_x(step):
        return at(z * X + lax.rem(x + 1 + step, X), dp)

    def remote(src, dst, send, recv, device_id):
        return pltpu.make_async_remote_copy(
            src_ref=src, dst_ref=dst, send_sem=send, recv_sem=recv, device_id=device_id, device_id_type=MESH
        )

    load_k = pltpu.make_async_copy(k_hbm, kv.at[0, 0:ROWS], in_sem.at[0])
    load_v = pltpu.make_async_copy(v_hbm, kv.at[1, 0:ROWS], in_sem.at[1])
    load_d = pltpu.make_async_copy(d_hbm, d, in_sem.at[2])
    load_w = pltpu.make_async_copy(w_hbm, w, in_sem.at[3])
    load_q = pltpu.make_async_copy(q_hbm, q, in_sem.at[4])
    for load in (load_k, load_v, load_d, load_w, load_q):
        load.start()
    barrier = pltpu.get_barrier_semaphore()
    partners = [right, left, twin, at_ya, at_yb] + fours
    partners += [at_z(step) for step in range(Z - 1)] + [at_x(step) for step in range(X - 1)]
    for partner in partners:
        pl.semaphore_signal(barrier, inc=1, device_id=partner, device_id_type=MESH)

    fill_bias(bias, seq)
    spread[...] = spread_matrix()

    matrix, scale = pool_matrix()
    pooled = []
    for part, load in ((0, load_k), (1, load_v)):
        load.wait()
        sums = dot_nn(matrix, kv[part, 0:ROWS, :]) * scale
        half = sums[0:112].astype(BF16)
        kv[part, OWN1:LEFT, :] = half[0:96]
        rim[0, part, 0:16] = kv[part, 0:16, :]
        rim[0, part, 16:32] = half[0:16]
        rim[0, part, 32:48] = half[64:80]
        rim[0, part, 48:64] = half[96:112]
        rim[1, part, 0:16] = kv[part, 112:128, :]
        rim[1, part, 16:32] = half[48:64]
        rim[1, part, 32:48] = half[80:96]
        rim[1, part, 48:64] = half[96:112]
        pooled.append(sums[112:120])
    four[...] = jnp.concatenate(pooled, axis=0).astype(BF16)

    pl.semaphore_wait(barrier, len(partners))

    rims = []
    for part in (0, 1):
        rims.append(
            remote(rim.at[0, part], kv.at[part, RIGHT:LEFT4], rim_s.at[2 * part], rim_r.at[2 * part], left)
        )
        rims.append(
            remote(rim.at[1, part], kv.at[part, LEFT:RIGHT], rim_s.at[2 * part + 1], rim_r.at[2 * part + 1], right)
        )
    sent_four = []
    for number, partner in enumerate(fours):
        slot = parity + (2 if number < 2 else 0)
        sent_four.append(remote(four, four_in.at[slot], four_s.at[number], four_r.at[slot], partner))
    for copy in rims[:2] + sent_four + rims[2:]:
        copy.start()

    load_d.wait()
    mine_rows = pl.ds(pl.multiple_of(core * ROWS, ROWS), ROWS)
    twin_columns = []
    for number, y_to in enumerate((y, ya, yb, yo)):
        columns = slice(number * PAIR, (number + 1) * PAIR)
        theirs = pl.ds(pl.multiple_of(y_to * 256 + (1 - core) * PAIR, PAIR), PAIR)
        copy = remote(
            d.at[:, theirs], pairs_d.at[mine_rows, columns], d2_s.at[number], d2_r.at[number], twin
        )
        copy.start()
        twin_columns.append(copy)
        ours = pl.ds(pl.multiple_of(y_to * 256 + core * PAIR, PAIR), PAIR)
        pairs_d[mine_rows, columns] = d[:, ours]

    load_w.wait()
    for column in range(0, WIDTH, 256):
        g[:, column : column + 256] = dot_nt(d[...], w[column : column + 256, :]).astype(BF16)
    load_q.wait()

    for copy in rims:
        copy.wait_recv()
    for number in range(4):
        remote(four, four_in.at[number], four_s.at[number], four_r.at[number], fours[number]).wait_recv()
    for side, row in ((0, LEFT4), (1, RIGHT4)):
        one = four_in[2 * side].astype(F32)
        two = four_in[2 * side + 1].astype(F32)
        for part in (0, 1):
            kv[part, row : row + 16, :] = jnp.concatenate(
                [one[8 * part : 8 * part + 8], two[8 * part : 8 * part + 8]], axis=0
            ).astype(BF16)
    for copy in twin_columns:
        copy.wait_recv()

    def lanes_of(step):
        return pl.ds(pl.multiple_of(lax.rem(z + 1 + step, PAIRS) * PAIR, PAIR), PAIR)

    mine_lanes = pl.ds(pl.multiple_of(core * ROWS, ROWS), ROWS)

    def copy_a(step):
        block = pairs_a.at[step, :, mine_lanes]
        return remote(block, block, a_s.at[step], a_r.at[step], twin)

    def copies_y1(step):
        return (
            remote(y1_out.at[step, 0], y1_in.at[step, 0], y1_s.at[2 * step], y1_r.at[2 * step], at_ya),
            remote(y1_out.at[step, 1], y1_in.at[step, 1], y1_s.at[2 * step + 1], y1_r.at[2 * step + 1], at_yb),
        )

    def copies_y2(step):
        return (
            remote(y2_out.at[step, 0], y2_in.at[step, 0], y2_s.at[2 * step], y2_r.at[2 * step], at_yb),
            remote(y2_out.at[step, 1], y2_in.at[step, 1], y2_s.at[2 * step + 1], y2_r.at[2 * step + 1], at_ya),
        )

    def copy_z(step):
        return remote(z_out.at[step], z_in.at[step], z_s.at[step], z_r.at[step], at_z(step))

    def forward(step):
        lanes = lanes_of(step)
        key_rows = kv[0, :, lanes]
        query_rows = two_heads(q[:, lanes], 0.125)
        scores = dot_nt(key_rows, query_rows) + bias[...]
        top = jnp.max(scores, axis=0, keepdims=True)
        exponent = jnp.exp(scores - top)
        weight = exponent * (1.0 / jnp.sum(exponent, axis=0, keepdims=True))
        weights[step] = weight
        attended = one_of_two(dot_tn(kv[1, :, lanes], weight.astype(BF16))).astype(BF16)
        pairs_a[step, :, mine_lanes] = attended
        copy_a(step).start()

    def project(step):
        copy_a(step).wait_recv()
        partial = dot_nn(pairs_a[step], pairs_d[...])
        kept[step] = partial[:, 0:128]
        kept2[step, 0:64] = partial[0:64, 256:384]
        kept2[step, 64:128] = partial[64:128, 128:256]
        y1_out[step, 0, 0:64] = partial[0:64, 128:256].astype(BF16)
        y1_out[step, 0, 64:128] = partial[0:64, 384:512].astype(BF16)
        y1_out[step, 1, 0:64] = partial[64:128, 256:384].astype(BF16)
        y1_out[step, 1, 64:128] = partial[64:128, 384:512].astype(BF16)
        for copy in copies_y1(step):
            copy.start()

    def fold_y1(step):
        for copy in copies_y1(step):
            copy.wait_recv()
        for half in (0, 1):
            rows = slice(64 * half, 64 * half + 64)
            kept[step, rows] = kept[step, rows] + y1_in[step, half, 0:64].astype(F32)
            y2_out[step, half] = (kept2[step, rows] + y1_in[step, half, 64:128].astype(F32)).astype(BF16)
        for copy in copies_y2(step):
            copy.start()

    def fold_y2(step):
        for copy in copies_y2(step):
            copy.wait_recv()
        for half in (0, 1):
            rows = slice(64 * half, 64 * half + 64)
            kept[step, rows] = kept[step, rows] + y2_in[step, half].astype(F32)

        @pl.when(step < PAIRS - 1)
        def _():
            z_out[step] = kept[step].astype(BF16)
            copy_z(step).start()

    def backward(step):
        lanes = lanes_of(step)
        key_rows = kv[0, :, lanes]
        value_rows = kv[1, :, lanes]
        query_rows = two_heads(q[:, lanes], 0.125)
        grad_rows = two_heads(g[:, lanes], 1.0)
        weight = weights[step]
        d_prob = dot_nt(value_rows, grad_rows)
        delta = jnp.sum(weight * d_prob, axis=0, keepdims=True)
        d_score = (weight * (d_prob - delta)).astype(BF16)
        d_query = one_of_two(dot_tn(key_rows, d_score)) * 0.125
        dq_ref[:, lanes] = d_query.T.astype(BF16)
        d_key = dot_nn(d_score, query_rows)
        d_value = dot_nn(weight.astype(BF16), grad_rows)
        for part, grad in ((0, d_key), (1, d_value)):
            own[part, :, lanes] = grad[0:ROWS]
            back[part, 0:64, lanes] = (grad[OWN1:OWN2] * 2.0 ** (-0.5)).astype(BF16)
            back[part, 64:96, lanes] = (grad[OWN2:LEFT] * 0.5).astype(BF16)
            for side, row in ((0, LEFT), (1, RIGHT)):
                for level in range(4):
                    piece = grad[row + 16 * level : row + 16 * level + 16] * 2.0 ** (-0.5 * level)
                    back_rim[side, part, 16 * level : 16 * level + 16, lanes] = piece.astype(BF16)
        for side, row in ((0, LEFT4), (1, RIGHT4)):
            for half in (0, 1):
                rows = slice(row + 8 * half, row + 8 * half + 8)
                both = jnp.concatenate([d_key[rows], d_value[rows]], axis=0) * 0.25
                back_four[2 * side + half, :, lanes] = both.astype(BF16)
        remote(
            back_rim.at[0, :, :, lanes], back.at[:, 96:160, lanes], back_s.at[0], back_r.at[0], left
        ).start()
        remote(
            back_rim.at[1, :, :, lanes], back.at[:, 160:224, lanes], back_s.at[1], back_r.at[1], right
        ).start()
        for number, partner in enumerate(fours):
            slot = parity + (2 if number < 2 else 0)
            remote(
                back_four.at[number, :, lanes],
                back_four_in.at[slot, :, lanes],
                bfour_s.at[number],
                bfour_r.at[slot],
                partner,
            ).start()

    def forward_step(step, carry):
        @pl.when(step >= 1)
        def _():
            project(step - 1)

        @pl.when(step >= 3)
        def _():
            fold_y1(step - 3)

        @pl.when(step >= 5)
        def _():
            fold_y2(step - 5)

        forward(step)
        return carry

    def backward_step(step, carry):
        @pl.when(step < 1)
        def _():
            project(step + 7)

        @pl.when(step < 3)
        def _():
            fold_y1(step + 5)

        @pl.when(step < 5)
        def _():
            fold_y2(step + 3)

        backward(step)
        return carry

    lax.fori_loop(0, PAIRS, forward_step, 0)
    lax.fori_loop(0, PAIRS, backward_step, 0)

    total = kept[PAIRS - 1]
    for step in range(Z - 1):
        copy_z(step).wait_recv()
        total = total + z_in[step].astype(F32)
    x_out[...] = total
    sent_x = []
    for step in range(X - 1):
        rows = pl.ds(pl.multiple_of(lax.rem(x + 1 + step, X) * 32, 32), 32)
        copy = remote(x_out.at[rows], x_in.at[step], x_s.at[step], x_r.at[step], at_x(step))
        copy.start()
        sent_x.append(copy)

    rim_left = remote(back_rim.at[0], back.at[:, 96:160], back_s.at[0], back_r.at[0], left)
    rim_right = remote(back_rim.at[1], back.at[:, 160:224], back_s.at[1], back_r.at[1], right)
    rim_left.wait_recv()
    rim_right.wait_recv()
    for number in range(4):
        remote(
            back_four.at[number], back_four_in.at[number], bfour_s.at[number], bfour_r.at[number], fours[number]
        ).wait_recv()
    for part, out in ((0, dk_ref), (1, dv_ref)):
        for column in range(0, WIDTH, 256):
            columns = slice(column, column + 256)
            rows4 = [back_four_in[number, :, columns].astype(F32)[8 * part : 8 * part + 8] for number in range(4)]
            back[part, 224:256, columns] = jnp.concatenate(rows4, axis=0).astype(BF16)
            out[:, columns] = (own[part, :, columns] + dot_nn(spread[...], back[part, :, columns])).astype(BF16)

    mine = x_out[pl.ds(pl.multiple_of(x * 32, 32), 32), :]
    for step in range(X - 1):
        sent_x[step].wait_recv()
        mine = mine + x_in[step]
    gw_ref[...] = mine * FACTOR

    for copy in rims + sent_four + twin_columns + sent_x + [rim_left, rim_right]:
        copy.wait_send()
    for number in range(4):
        remote(
            back_four.at[number], back_four_in.at[number], bfour_s.at[number], bfour_r.at[number], fours[number]
        ).wait_send()

    def wait_sends(step, carry):
        copy_a(step).wait_send()
        for copy in copies_y1(step) + copies_y2(step):
            copy.wait_send()

        @pl.when(step < PAIRS - 1)
        def _():
            copy_z(step).wait_send()

        return carry

    lax.fori_loop(0, PAIRS, wait_sends, 0)


def on_device(queries, keys, values, d_out, w_out):
    dma = pltpu.SemaphoreType.DMA
    any_space = pl.BlockSpec(memory_space=pl.ANY)
    vmem = pl.BlockSpec(memory_space=pltpu.VMEM)
    rows_shape = jax.ShapeDtypeStruct((ROWS, WIDTH), BF16)
    d_queries, d_keys, d_values, grad_w = pl.pallas_call(
        kernel,
        out_shape=(rows_shape, rows_shape, rows_shape, jax.ShapeDtypeStruct((32, 128), F32)),
        in_specs=[any_space] * 5,
        out_specs=(vmem,) * 4,
        scratch_shapes=[
            pltpu.VMEM((ROWS, WIDTH), BF16),
            pltpu.VMEM((ROWS, WIDTH), BF16),
            pltpu.VMEM((WIDTH, WIDTH), BF16),
            pltpu.VMEM((ROWS, WIDTH), BF16),
            pltpu.VMEM((2, KEYS, WIDTH), BF16),
            pltpu.VMEM((KEYS, 2 * ROWS), F32),
            pltpu.VMEM((ROWS, 256), BF16),
            pltpu.VMEM((2, 2, 64, WIDTH), BF16),
            pltpu.VMEM((16, WIDTH), BF16),
            pltpu.VMEM((4, 16, WIDTH), BF16),
            pltpu.VMEM((PAIRS, KEYS, 2 * ROWS), F32),
            pltpu.VMEM((2, ROWS, WIDTH), F32),
            pltpu.VMEM((2, 256, WIDTH), BF16),
            pltpu.VMEM((2, 2, 64, WIDTH), BF16),
            pltpu.VMEM((4, 16, WIDTH), BF16),
            pltpu.VMEM((4, 16, WIDTH), BF16),
            pltpu.VMEM((PAIRS, PAIR, 2 * ROWS), BF16),
            pltpu.VMEM((2 * ROWS, 512), BF16),
            pltpu.VMEM((PAIRS, 128, 128), F32),
            pltpu.VMEM((PAIRS, 128, 128), F32),
            pltpu.VMEM((PAIRS, 2, 128, 128), BF16),
            pltpu.VMEM((PAIRS, 2, 128, 128), BF16),
            pltpu.VMEM((PAIRS, 2, 64, 128), BF16),
            pltpu.VMEM((PAIRS, 2, 64, 128), BF16),
            pltpu.VMEM((Z - 1, 128, 128), BF16),
            pltpu.VMEM((Z - 1, 128, 128), BF16),
            pltpu.VMEM((128, 128), F32),
            pltpu.VMEM((X - 1, 32, 128), F32),
            dma((5,)),
            dma((4,)), dma((4,)),
            dma((4,)), dma((4,)),
            dma((4,)), dma((4,)),
            dma((PAIRS,)), dma((PAIRS,)),
            dma((2 * PAIRS,)), dma((2 * PAIRS,)),
            dma((2 * PAIRS,)), dma((2 * PAIRS,)),
            dma((Z - 1,)), dma((Z - 1,)),
            dma((X - 1,)), dma((X - 1,)),
            dma((2,)), dma((2,)),
            dma((4,)), dma((4,)),
        ],
        compiler_params=pltpu.CompilerParams(
            collective_id=0, has_side_effects=True, vmem_limit_bytes=48 * 1024 * 1024
        ),
    )(queries[0], keys[0], values[0], d_out[0], w_out)
    return d_queries[None], d_keys[None], d_values[None], grad_w


def solution(mesh):
    placed = P("dp", "seq", None)
    return jax.shard_map(
        on_device,
        mesh=mesh,
        in_specs=(placed, placed, placed, placed, P()),
        out_specs=(placed, placed, placed, P("seq", "dp")),
        check_vma=False,
    )
```

```python
import jax
import jax.numpy as jnp
from jax import lax
from jax.experimental import pallas as pl
from jax.experimental.pallas import tpu as pltpu
from jax.sharding import PartitionSpec as P

ROWS = 128
WIDTH = 1024
PAIR = 128
PAIRS = 8
KEYS = 384
N_SEQ = 32
X, Z = 4, 8
FACTOR = 32768 ** (-0.5)
AHEAD = 3
VMEM_BYTES = 63 * 1024 * 1024
MESH = pl.DeviceIdType.MESH
F32 = jnp.float32
BF16 = jnp.bfloat16

OWN1, OWN2, LEFT, RIGHT, LEFT4, RIGHT4 = 128, 192, 224, 288, 352, 368


def dot_nt(a, b):
    return lax.dot_general(a, b, (((1,), (1,)), ((), ())), preferred_element_type=F32)


def dot_tn(a, b):
    return lax.dot_general(a, b, (((0,), (0,)), ((), ())), preferred_element_type=F32)


def dot_nn(a, b):
    return lax.dot_general(a, b, (((1,), (0,)), ((), ())), preferred_element_type=F32)


def two_heads(block, scale):
    lane = lax.broadcasted_iota(jnp.int32, (1, PAIR), 1)
    first = jnp.where(lane < 64, scale, 0.0).astype(BF16)
    second = jnp.where(lane < 64, 0.0, scale).astype(BF16)
    return jnp.concatenate([block * first, block * second], axis=0)


def one_of_two(both):
    row = lax.broadcasted_iota(jnp.int32, (PAIR, ROWS), 0)
    return jnp.where(row < 64, both[:, :ROWS], both[:, ROWS:])


def pool_matrix():
    row = lax.broadcasted_iota(jnp.int32, (ROWS, ROWS), 0)
    token = lax.broadcasted_iota(jnp.int32, (ROWS, ROWS), 1)
    level = jnp.where(row < 64, 1, jnp.where(row < 96, 2, jnp.where(row < 112, 3, 4)))
    base = jnp.where(row < 64, 0, jnp.where(row < 96, 64, jnp.where(row < 112, 96, 112)))
    matrix = jnp.where(lax.shift_right_logical(token, level) == row - base, 1.0, 0.0).astype(BF16)
    row = lax.broadcasted_iota(jnp.int32, (ROWS, 1), 0)
    scale = jnp.where(
        row < 64, 2.0 ** (-0.5), jnp.where(row < 96, 0.5, jnp.where(row < 112, 2.0 ** (-1.5), 0.25))
    ).astype(F32)
    return matrix, scale


def spread_matrix():
    token = lax.broadcasted_iota(jnp.int32, (ROWS, 256), 0)
    row = lax.broadcasted_iota(jnp.int32, (ROWS, 256), 1)
    in_rim = lax.rem(row - 96, 64)
    rim_level = in_rim // 16
    within = lax.rem(in_rim, 16)
    rim_last = jnp.where(rim_level == 0, 112, jnp.where(rim_level == 1, 48, jnp.where(rim_level == 2, 16, 0)))
    level = jnp.where(row < 64, 1, jnp.where(row < 96, 2, jnp.where(row < 224, rim_level, 4)))
    target = jnp.where(
        row < 64,
        row,
        jnp.where(
            row < 96,
            row - 64,
            jnp.where(row < 160, rim_last + within, jnp.where(row < 224, within, lax.rem(row - 224, 8))),
        ),
    )
    return jnp.where(lax.shift_right_logical(token, level) == target, 1.0, 0.0).astype(BF16)


def fill_bias(bias, device):
    token = lax.rem(lax.broadcasted_iota(jnp.int32, (16, 2 * ROWS), 1), ROWS)
    not_first = device > 0
    not_last = device < N_SEQ - 1

    def put(row, valid):
        bias[row : row + 16, :] = jnp.where(valid, 0.0, -1e30).astype(F32)

    for block in range(8):
        near = token // 16 - block
        put(16 * block, (near >= -1) & (near <= 1))
    for block in range(4):
        near = token // 32 - block
        put(OWN1 + 16 * block, (near == -1) | (near == 1))
    for block in range(2):
        put(OWN2 + 16 * block, token // 64 != block)
    for level in range(4):
        span = 16 * 2**level
        put(LEFT + 16 * level, (token < span) & not_first)
        put(RIGHT + 16 * level, (token >= ROWS - span) & not_last)
    always = token >= 0
    put(LEFT4, always & (device >= 2))
    put(RIGHT4, always & (device < N_SEQ - 2))


def kernel(
    q_hbm, k_hbm, v_hbm, d_hbm, w_hbm,
    dq_hbm, dk_hbm, dv_hbm, gw_hbm,
    dq_ref, dk_ref, dv_ref, gw_ref, q, d, w, g, kv, bias, spread,
    rim, four, four_in,
    weights, own, back, back_rim, back_four, back_four_in,
    pairs_a, pairs_d, kept, kept2, y1_out, y1_in, y2_out, y2_in, z_out, z_in,
    in_sem, out_sem, rim_s, rim_r, four_s, four_r, d2_s, d2_r, a_s, a_r, y1_s, y1_r, y2_s, y2_r,
    z_s, z_r, back_s, back_r, bfour_s, bfour_r,
):
    seq = lax.axis_index("seq")
    dp = lax.axis_index("dp")
    z, x = lax.div(seq, X), lax.rem(seq, X)
    y, core = lax.div(dp, 2), lax.rem(dp, 2)
    ya = y + 1 - 2 * lax.rem(y, 2)
    yb = 3 - y
    yo = 3 - ya
    pair_of = lax.div(seq, 2)
    parity = lax.rem(seq, 2)

    def at(seq_to, dp_to):
        return {"seq": seq_to, "dp": dp_to}

    right = at(lax.rem(seq + 1, N_SEQ), dp)
    left = at(lax.rem(seq + N_SEQ - 1, N_SEQ), dp)
    twin = at(seq, 2 * y + 1 - core)
    at_ya = at(seq, 2 * ya + core)
    at_yb = at(seq, 2 * yb + core)
    fours = []
    for side in (0, 1):
        block = lax.rem(pair_of + (N_SEQ // 2 - 1 if side == 0 else 1), N_SEQ // 2)
        for part in (0, 1):
            fours.append(at(2 * block + part, dp))

    def owner(step, apart):
        return at(lax.rem(z + 1 + step, Z) * X + lax.rem(x + apart, X), dp)

    def remote(src, dst, send, recv, device_id):
        return pltpu.make_async_remote_copy(
            src_ref=src, dst_ref=dst, send_sem=send, recv_sem=recv, device_id=device_id, device_id_type=MESH
        )

    load_k = pltpu.make_async_copy(k_hbm, kv.at[0, 0:ROWS], in_sem.at[0])
    load_v = pltpu.make_async_copy(v_hbm, kv.at[1, 0:ROWS], in_sem.at[1])
    load_d = pltpu.make_async_copy(d_hbm, d, in_sem.at[2])
    load_w = pltpu.make_async_copy(w_hbm, w, in_sem.at[3])
    load_q = pltpu.make_async_copy(q_hbm, q, in_sem.at[4])
    for load in (load_k, load_v, load_d, load_w, load_q):
        load.start()
    barrier = pltpu.get_barrier_semaphore()
    partners = [right, left, twin, at_ya, at_yb] + fours
    for partner in partners:
        pl.semaphore_signal(barrier, inc=1, device_id=partner, device_id_type=MESH)

    def greet(number, carry):
        pl.semaphore_signal(barrier, inc=1, device_id=at(lax.rem(seq + number, N_SEQ), dp), device_id_type=MESH)
        return carry

    lax.fori_loop(1, N_SEQ, greet, 0)

    fill_bias(bias, seq)
    spread[...] = spread_matrix()

    matrix, scale = pool_matrix()
    pooled = []
    for part, load in ((0, load_k), (1, load_v)):
        load.wait()
        sums = dot_nn(matrix, kv[part, 0:ROWS, :]) * scale
        half = sums[0:112].astype(BF16)
        kv[part, OWN1:LEFT, :] = half[0:96]
        rim[0, part, 0:16] = kv[part, 0:16, :]
        rim[0, part, 16:32] = half[0:16]
        rim[0, part, 32:48] = half[64:80]
        rim[0, part, 48:64] = half[96:112]
        rim[1, part, 0:16] = kv[part, 112:128, :]
        rim[1, part, 16:32] = half[48:64]
        rim[1, part, 32:48] = half[80:96]
        rim[1, part, 48:64] = half[96:112]
        pooled.append(sums[112:120])
    four[...] = jnp.concatenate(pooled, axis=0).astype(BF16)

    load_d.wait()
    load_w.wait()
    for column in range(0, WIDTH, 256):
        g[:, column : column + 256] = dot_nt(d[...], w[column : column + 256, :]).astype(BF16)
    load_q.wait()
    mine_rows = pl.ds(pl.multiple_of(core * ROWS, ROWS), ROWS)
    for number, y_to in enumerate((y, ya, yb, yo)):
        ours = pl.ds(pl.multiple_of(y_to * 256 + core * PAIR, PAIR), PAIR)
        pairs_d[mine_rows, number * PAIR : (number + 1) * PAIR] = d[:, ours]

    pl.semaphore_wait(barrier, len(partners) + N_SEQ - 1)

    sent_four = []
    for number, partner in enumerate(fours):
        slot = parity + (2 if number < 2 else 0)
        sent_four.append(remote(four, four_in.at[slot], four_s.at[number], four_r.at[slot], partner))
    for copy in sent_four:
        copy.start()

    z_left = lax.div(lax.rem(seq + N_SEQ - 1, N_SEQ), X)
    z_right = lax.div(lax.rem(seq + 1, N_SEQ), X)

    def send_rims(step):
        for side, z_to, row, partner in ((0, z_left, RIGHT, left), (1, z_right, LEFT, right)):
            lanes = pl.ds(pl.multiple_of(lax.rem(z_to + 1 + step, PAIRS) * PAIR, PAIR), PAIR)
            remote(
                rim.at[side, :, :, lanes],
                kv.at[:, row : row + 64, lanes],
                rim_s.at[side],
                rim_r.at[side * PAIRS + step],
                partner,
            ).start()

    def wait_rims(step):
        lanes = lanes_of(step)
        for side, row, partner in ((0, RIGHT, left), (1, LEFT, right)):
            remote(
                rim.at[side, :, :, lanes],
                kv.at[:, row : row + 64, lanes],
                rim_s.at[side],
                rim_r.at[side * PAIRS + step],
                partner,
            ).wait_recv()

    for step in range(AHEAD):
        send_rims(step)

    twin_columns = []
    for number, y_to in enumerate((y, ya, yb, yo)):
        columns = slice(number * PAIR, (number + 1) * PAIR)
        theirs = pl.ds(pl.multiple_of(y_to * 256 + (1 - core) * PAIR, PAIR), PAIR)
        copy = remote(
            d.at[:, theirs], pairs_d.at[mine_rows, columns], d2_s.at[number], d2_r.at[number], twin
        )
        copy.start()
        twin_columns.append(copy)

    for number in range(4):
        remote(four, four_in.at[number], four_s.at[number], four_r.at[number], fours[number]).wait_recv()
    for side, row in ((0, LEFT4), (1, RIGHT4)):
        one = four_in[2 * side].astype(F32)
        two = four_in[2 * side + 1].astype(F32)
        for part in (0, 1):
            kv[part, row : row + 16, :] = jnp.concatenate(
                [one[8 * part : 8 * part + 8], two[8 * part : 8 * part + 8]], axis=0
            ).astype(BF16)
    for copy in twin_columns:
        copy.wait_recv()

    def lanes_of(step):
        return pl.ds(pl.multiple_of(lax.rem(z + 1 + step, PAIRS) * PAIR, PAIR), PAIR)

    mine_lanes = pl.ds(pl.multiple_of(core * ROWS, ROWS), ROWS)

    def copy_a(step):
        block = pairs_a.at[step, :, mine_lanes]
        return remote(block, block, a_s.at[step], a_r.at[step], twin)

    def copies_y1(step):
        return (
            remote(y1_out.at[step, 0], y1_in.at[step, 0], y1_s.at[2 * step], y1_r.at[2 * step], at_ya),
            remote(y1_out.at[step, 1], y1_in.at[step, 1], y1_s.at[2 * step + 1], y1_r.at[2 * step + 1], at_yb),
        )

    def copies_y2(step):
        return (
            remote(y2_out.at[step, 0], y2_in.at[step, 0], y2_s.at[2 * step], y2_r.at[2 * step], at_yb),
            remote(y2_out.at[step, 1], y2_in.at[step, 1], y2_s.at[2 * step + 1], y2_r.at[2 * step + 1], at_ya),
        )

    def copy_z(step, apart, slot):
        rows = pl.ds(pl.multiple_of(lax.rem(x + apart, X) * 32, 32), 32)
        return remote(z_out.at[step, rows], z_in.at[slot], z_s.at[0], z_r.at[0], owner(step, apart))

    def forward(step):
        lanes = lanes_of(step)
        key_rows = kv[0, :, lanes]
        query_rows = two_heads(q[:, lanes], 0.125)
        scores = dot_nt(key_rows, query_rows) + bias[...]
        top = jnp.max(scores, axis=0, keepdims=True)
        exponent = jnp.exp(scores - top)
        weight = exponent * (1.0 / jnp.sum(exponent, axis=0, keepdims=True))
        weights[step] = weight
        attended = one_of_two(dot_tn(kv[1, :, lanes], weight.astype(BF16))).astype(BF16)
        pairs_a[step, :, mine_lanes] = attended
        copy_a(step).start()

    def project(step):
        copy_a(step).wait_recv()
        partial = dot_nn(pairs_a[step], pairs_d[...])
        kept[step] = partial[:, 0:128]
        kept2[step, 0:64] = partial[0:64, 256:384]
        kept2[step, 64:128] = partial[64:128, 128:256]
        y1_out[step, 0, 0:64] = partial[0:64, 128:256].astype(BF16)
        y1_out[step, 0, 64:128] = partial[0:64, 384:512].astype(BF16)
        y1_out[step, 1, 0:64] = partial[64:128, 256:384].astype(BF16)
        y1_out[step, 1, 64:128] = partial[64:128, 384:512].astype(BF16)
        for copy in copies_y1(step):
            copy.start()

    def fold_y1(step):
        for copy in copies_y1(step):
            copy.wait_recv()
        for half in (0, 1):
            rows = slice(64 * half, 64 * half + 64)
            kept[step, rows] = kept[step, rows] + y1_in[step, half, 0:64].astype(F32)
            y2_out[step, half] = (kept2[step, rows] + y1_in[step, half, 64:128].astype(F32)).astype(BF16)
        for copy in copies_y2(step):
            copy.start()

    def fold_y2(step):
        for copy in copies_y2(step):
            copy.wait_recv()
        for half in (0, 1):
            rows = slice(64 * half, 64 * half + 64)
            kept[step, rows] = kept[step, rows] + y2_in[step, half].astype(F32)

        z_out[step] = kept[step].astype(BF16)

        @pl.when(step < PAIRS - 1)
        def _():
            copy_z(step, 0, 4 * step).start()

        for apart in range(1, X):
            copy_z(step, apart, 4 * step + apart - lax.div(step, PAIRS - 1)).start()

    def backward(step):
        lanes = lanes_of(step)
        key_rows = kv[0, :, lanes]
        value_rows = kv[1, :, lanes]
        query_rows = two_heads(q[:, lanes], 0.125)
        grad_rows = two_heads(g[:, lanes], 1.0)
        weight = weights[step]
        d_prob = dot_nt(value_rows, grad_rows)
        delta = jnp.sum(weight * d_prob, axis=0, keepdims=True)
        d_score = (weight * (d_prob - delta)).astype(BF16)
        d_query = one_of_two(dot_tn(key_rows, d_score)) * 0.125
        dq_ref[:, lanes] = d_query.T.astype(BF16)
        d_key = dot_nn(d_score, query_rows)
        d_value = dot_nn(weight.astype(BF16), grad_rows)
        for part, grad in ((0, d_key), (1, d_value)):
            own[part, :, lanes] = grad[0:ROWS]
            back[part, 0:64, lanes] = (grad[OWN1:OWN2] * 2.0 ** (-0.5)).astype(BF16)
            back[part, 64:96, lanes] = (grad[OWN2:LEFT] * 0.5).astype(BF16)
            for side, row in ((0, LEFT), (1, RIGHT)):
                for level in range(4):
                    piece = grad[row + 16 * level : row + 16 * level + 16] * 2.0 ** (-0.5 * level)
                    back_rim[side, part, 16 * level : 16 * level + 16, lanes] = piece.astype(BF16)
        for side, row in ((0, LEFT4), (1, RIGHT4)):
            for half in (0, 1):
                rows = slice(row + 8 * half, row + 8 * half + 8)
                both = jnp.concatenate([d_key[rows], d_value[rows]], axis=0) * 0.25
                back_four[2 * side + half, :, lanes] = both.astype(BF16)
        remote(
            back_rim.at[0, :, :, lanes], back.at[:, 96:160, lanes], back_s.at[0], back_r.at[0], left
        ).start()
        remote(
            back_rim.at[1, :, :, lanes], back.at[:, 160:224, lanes], back_s.at[1], back_r.at[1], right
        ).start()
        for number, partner in enumerate(fours):
            slot = parity + (2 if number < 2 else 0)
            remote(
                back_four.at[number, :, lanes],
                back_four_in.at[slot, :, lanes],
                bfour_s.at[number],
                bfour_r.at[slot],
                partner,
            ).start()

    def forward_step(step, carry):
        wait_rims(step)

        @pl.when(step < PAIRS - AHEAD)
        def _():
            send_rims(step + AHEAD)

        forward(step)

        @pl.when(step >= 2)
        def _():
            project(step - 2)

        @pl.when(step >= 6)
        def _():
            fold_y1(step - 6)

        return carry

    def backward_step(step, carry):
        backward(step)

        @pl.when(step < 2)
        def _():
            project(step + 6)

        @pl.when(step < 6)
        def _():
            fold_y1(step + 2)

        @pl.when(step >= 1)
        def _():
            fold_y2(step - 1)

        return carry

    lax.fori_loop(0, PAIRS, forward_step, 0)
    lax.fori_loop(0, PAIRS, backward_step, 0)
    fold_y2(PAIRS - 1)
    store_q = pltpu.make_async_copy(dq_ref, dq_hbm, out_sem.at[0])
    store_q.start()

    rim_left = remote(back_rim.at[0], back.at[:, 96:160], back_s.at[0], back_r.at[0], left)
    rim_right = remote(back_rim.at[1], back.at[:, 160:224], back_s.at[1], back_r.at[1], right)
    rim_left.wait_recv()
    rim_right.wait_recv()
    for number in range(4):
        remote(
            back_four.at[number], back_four_in.at[number], bfour_s.at[number], bfour_r.at[number], fours[number]
        ).wait_recv()
    stores = [store_q]
    for part, out in ((0, dk_ref), (1, dv_ref)):
        for column in range(0, WIDTH, 256):
            columns = slice(column, column + 256)
            rows4 = [back_four_in[number, :, columns].astype(F32)[8 * part : 8 * part + 8] for number in range(4)]
            back[part, 224:256, columns] = jnp.concatenate(rows4, axis=0).astype(BF16)
            out[:, columns] = (own[part, :, columns] + dot_nn(spread[...], back[part, :, columns])).astype(BF16)
        store = pltpu.make_async_copy(out, (dk_hbm, dv_hbm)[part], out_sem.at[1 + part])
        store.start()
        stores.append(store)

    all_z = remote(z_in, z_in, z_s.at[0], z_r.at[0], right)
    all_z.wait_recv()
    mine = kept[PAIRS - 1, pl.ds(pl.multiple_of(x * 32, 32), 32), :]
    gw_ref[...] = (mine + jnp.sum(z_in[...].astype(F32), axis=0)) * FACTOR
    store = pltpu.make_async_copy(gw_ref, gw_hbm, out_sem.at[3])
    store.start()
    stores.append(store)

    sent_rims = [
        remote(rim.at[side], kv.at[:, LEFT:RIGHT], rim_s.at[side], rim_r.at[0], right) for side in (0, 1)
    ]
    for copy in sent_rims + sent_four + twin_columns + [rim_left, rim_right, all_z]:
        copy.wait_send()
    for number in range(4):
        remote(
            back_four.at[number], back_four_in.at[number], bfour_s.at[number], bfour_r.at[number], fours[number]
        ).wait_send()

    def wait_sends(step, carry):
        copy_a(step).wait_send()
        for copy in copies_y1(step) + copies_y2(step):
            copy.wait_send()
        return carry

    lax.fori_loop(0, PAIRS, wait_sends, 0)
    for store in stores:
        store.wait()


def hand_on(*refs):
    given, results, held, sems = refs[0:4], refs[4:8], refs[8:12], refs[12]
    loads = [pltpu.make_async_copy(given[i], held[i], sems.at[i]) for i in range(4)]
    stores = [pltpu.make_async_copy(held[i], results[i], sems.at[4 + i]) for i in range(4)]
    for load in loads:
        load.start()
    for load, store in zip(loads, stores):
        load.wait()
        store.start()
    for store in stores:
        store.wait()


def on_device(queries, keys, values, d_out, w_out):
    dma = pltpu.SemaphoreType.DMA
    any_space = pl.BlockSpec(memory_space=pl.ANY)
    rows_shape = jax.ShapeDtypeStruct((ROWS, WIDTH), BF16)
    grad_shape = jax.ShapeDtypeStruct((32, 128), F32)
    results = (rows_shape, rows_shape, rows_shape, grad_shape)
    held = [pltpu.VMEM(result.shape, result.dtype) for result in results]
    outs = pl.pallas_call(
        kernel,
        out_shape=results,
        in_specs=[any_space] * 5,
        out_specs=(any_space,) * 4,
        scratch_shapes=held
        + [
            pltpu.VMEM((ROWS, WIDTH), BF16),
            pltpu.VMEM((ROWS, WIDTH), BF16),
            pltpu.VMEM((WIDTH, WIDTH), BF16),
            pltpu.VMEM((ROWS, WIDTH), BF16),
            pltpu.VMEM((2, KEYS, WIDTH), BF16),
            pltpu.VMEM((KEYS, 2 * ROWS), F32),
            pltpu.VMEM((ROWS, 256), BF16),
            pltpu.VMEM((2, 2, 64, WIDTH), BF16),
            pltpu.VMEM((16, WIDTH), BF16),
            pltpu.VMEM((4, 16, WIDTH), BF16),
            pltpu.VMEM((PAIRS, KEYS, 2 * ROWS), F32),
            pltpu.VMEM((2, ROWS, WIDTH), F32),
            pltpu.VMEM((2, 256, WIDTH), BF16),
            pltpu.VMEM((2, 2, 64, WIDTH), BF16),
            pltpu.VMEM((4, 16, WIDTH), BF16),
            pltpu.VMEM((4, 16, WIDTH), BF16),
            pltpu.VMEM((PAIRS, PAIR, 2 * ROWS), BF16),
            pltpu.VMEM((2 * ROWS, 512), BF16),
            pltpu.VMEM((PAIRS, 128, 128), F32),
            pltpu.VMEM((PAIRS, 128, 128), F32),
            pltpu.VMEM((PAIRS, 2, 128, 128), BF16),
            pltpu.VMEM((PAIRS, 2, 128, 128), BF16),
            pltpu.VMEM((PAIRS, 2, 64, 128), BF16),
            pltpu.VMEM((PAIRS, 2, 64, 128), BF16),
            pltpu.VMEM((PAIRS, 128, 128), BF16),
            pltpu.VMEM((N_SEQ - 1, 32, 128), BF16),
            dma((5,)),
            dma((4,)),
            dma((2,)), dma((2 * PAIRS,)),
            dma((4,)), dma((4,)),
            dma((4,)), dma((4,)),
            dma((PAIRS,)), dma((PAIRS,)),
            dma((2 * PAIRS,)), dma((2 * PAIRS,)),
            dma((2 * PAIRS,)), dma((2 * PAIRS,)),
            dma((1,)), dma((1,)),
            dma((2,)), dma((2,)),
            dma((4,)), dma((4,)),
        ],
        compiler_params=pltpu.CompilerParams(
            collective_id=0, has_side_effects=True, vmem_limit_bytes=VMEM_BYTES
        ),
    )(queries[0], keys[0], values[0], d_out[0], w_out)
    d_queries, d_keys, d_values, grad_w = pl.pallas_call(
        hand_on,
        out_shape=results,
        in_specs=[any_space] * 4,
        out_specs=(any_space,) * 4,
        scratch_shapes=held + [dma((8,))],
        compiler_params=pltpu.CompilerParams(vmem_limit_bytes=VMEM_BYTES),
    )(*outs)
    return d_queries[None], d_keys[None], d_values[None], grad_w


def solution(mesh):
    placed = P("dp", "seq", None)
    return jax.shard_map(
        on_device,
        mesh=mesh,
        in_specs=(placed, placed, placed, placed, P()),
        out_specs=(placed, placed, placed, P("seq", "dp")),
        check_vma=False,
    )
```

```python
import jax
import jax.numpy as jnp
from jax import lax
from jax.experimental import pallas as pl
from jax.experimental.pallas import tpu as pltpu
from jax.sharding import PartitionSpec as P

ROWS = 128
WIDTH = 1024
PAIR = 128
PAIRS = 8
KEYS = 384
N_SEQ = 32
X, Z = 4, 8
FACTOR = 32768 ** (-0.5)
STEPS = 4
SENT = 80
WIDE = 256
VMEM_BYTES = 63 * 1024 * 1024
MESH = pl.DeviceIdType.MESH
F32 = jnp.float32
BF16 = jnp.bfloat16

OWN1, OWN2, LEFT, RIGHT, LEFT4, RIGHT4 = 128, 192, 224, 288, 352, 368


def dot_nt(a, b):
    return lax.dot_general(a, b, (((1,), (1,)), ((), ())), preferred_element_type=F32)


def dot_tn(a, b):
    return lax.dot_general(a, b, (((0,), (0,)), ((), ())), preferred_element_type=F32)


def dot_nn(a, b):
    return lax.dot_general(a, b, (((1,), (0,)), ((), ())), preferred_element_type=F32)


def two_heads(block, scale):
    lane = lax.broadcasted_iota(jnp.int32, (1, PAIR), 1)
    first = jnp.where(lane < 64, scale, 0.0).astype(BF16)
    second = jnp.where(lane < 64, 0.0, scale).astype(BF16)
    return jnp.concatenate([block * first, block * second], axis=0)


def one_of_two(both):
    row = lax.broadcasted_iota(jnp.int32, (PAIR, ROWS), 0)
    return jnp.where(row < 64, both[:, :ROWS], both[:, ROWS:])


def pool_matrix():
    row = lax.broadcasted_iota(jnp.int32, (ROWS, ROWS), 0)
    token = lax.broadcasted_iota(jnp.int32, (ROWS, ROWS), 1)
    level = jnp.where(row < 64, 1, jnp.where(row < 96, 2, jnp.where(row < 112, 3, 4)))
    base = jnp.where(row < 64, 0, jnp.where(row < 96, 64, jnp.where(row < 112, 96, 112)))
    matrix = jnp.where(lax.shift_right_logical(token, level) == row - base, 1.0, 0.0).astype(BF16)
    row = lax.broadcasted_iota(jnp.int32, (ROWS, 1), 0)
    scale = jnp.where(
        row < 64, 2.0 ** (-0.5), jnp.where(row < 96, 0.5, jnp.where(row < 112, 2.0 ** (-1.5), 0.25))
    ).astype(F32)
    return matrix, scale


def rim_row(row, side):
    level = lax.rem(row, 64) // 16
    within = lax.rem(row, 16)
    if side == 0:
        within = within + jnp.where(level == 0, 112, jnp.where(level == 1, 48, jnp.where(level == 2, 16, 0)))
    return row // 64, level, within


def sent_row(row, side):
    fine = row < 32
    level = jnp.where(fine, 0, (row - 16) // 16)
    part = jnp.where(fine, row // 16, lax.rem(row, 16) // 8)
    within = jnp.where(fine, lax.rem(row, 16), lax.rem(row, 8))
    if side == 0:
        base = jnp.where(fine, 112, jnp.where(level == 1, 48, jnp.where(level == 2, 16, 0)))
    else:
        base = jnp.where(fine, 0, 8)
    return part, level, lax.shift_left(base + within, level)


def rim_matrix(shape, rim_axis, side):
    part, level, position = rim_row(lax.broadcasted_iota(jnp.int32, shape, rim_axis), side)
    from_part, _, first = sent_row(lax.broadcasted_iota(jnp.int32, shape, 1 - rim_axis), side)
    covered = (part == from_part) & (lax.shift_right_logical(first, level) == position)
    return jnp.where(covered, 1.0, 0.0).astype(BF16)


def level_scale(level):
    return jnp.where(
        level == 0, 1.0, jnp.where(level == 1, 2.0 ** (-0.5), jnp.where(level == 2, 0.5, 2.0 ** (-1.5)))
    ).astype(F32)


def rim_scale(side):
    _, level, position = rim_row(lax.broadcasted_iota(jnp.int32, (ROWS, 1), 0), side)
    token = lax.shift_left(position, level)
    if side == 0:
        source = jnp.where(token >= 112, 0, jnp.where(token >= 96, 1, jnp.where(token >= 64, 2, 3)))
    else:
        source = jnp.where(token < 16, 0, jnp.where(token < 32, 1, jnp.where(token < 64, 2, 3)))
    return level_scale(level - source)


def spread_matrix():
    token = lax.broadcasted_iota(jnp.int32, (ROWS, ROWS), 0)
    row = lax.broadcasted_iota(jnp.int32, (ROWS, ROWS), 1)
    level = jnp.where(row < 64, 1, jnp.where(row < 96, 2, 4))
    target = jnp.where(row < 64, row, jnp.where(row < 96, row - 64, lax.rem(row - 96, 8)))
    return jnp.where(lax.shift_right_logical(token, level) == target, 1.0, 0.0).astype(BF16)


def spread_sent(part):
    columns = []
    for side in (0, 1):
        token = lax.broadcasted_iota(jnp.int32, (ROWS, SENT), 0)
        of_part, level, first = sent_row(lax.broadcasted_iota(jnp.int32, (ROWS, SENT), 1), side)
        same = lax.shift_right_logical(token, level) == lax.shift_right_logical(first, level)
        columns.append(jnp.where((of_part == part) & same, 1.0, 0.0))
    return columns


def fill_bias(bias, device):
    token = lax.rem(lax.broadcasted_iota(jnp.int32, (16, 2 * ROWS), 1), ROWS)
    not_first = device > 0
    not_last = device < N_SEQ - 1

    def put(row, valid):
        bias[row : row + 16, :] = jnp.where(valid, 0.0, -1e30).astype(F32)

    for block in range(8):
        near = token // 16 - block
        put(16 * block, (near >= -1) & (near <= 1))
    for block in range(4):
        near = token // 32 - block
        put(OWN1 + 16 * block, (near == -1) | (near == 1))
    for block in range(2):
        put(OWN2 + 16 * block, token // 64 != block)
    for level in range(4):
        span = 16 * 2**level
        put(LEFT + 16 * level, (token < span) & not_first)
        put(RIGHT + 16 * level, (token >= ROWS - span) & not_last)
    always = token >= 0
    put(LEFT4, always & (device >= 2))
    put(RIGHT4, always & (device < N_SEQ - 2))


def kernel(
    q_hbm, k_hbm, v_hbm, d_hbm, w_hbm,
    dq_hbm, dk_hbm, dv_hbm, gw_hbm,
    dq_ref, dk_ref, dv_ref, gw_ref, q, d, w, g, kv, bias, spread, spread_back, unfold, fold,
    rim, rim_in, four, four_in,
    weights, weights_half, grad_scores, own, back, back_in, back_rim, back_four, back_four_in,
    pairs_a, pairs_d, kept, kept2, y1_out, y1_in, y2_out, y2_in, z_out, z_in,
    in_sem, out_sem, rim_s, rim_r, four_s, four_r, d2_s, d2_r, a_s, a_r, y1_s, y1_r, y2_s, y2_r,
    z_s, z_r, back_s, back_r, bfour_s, bfour_r,
):
    seq = lax.axis_index("seq")
    dp = lax.axis_index("dp")
    z, x = lax.div(seq, X), lax.rem(seq, X)
    y, core = lax.div(dp, 2), lax.rem(dp, 2)
    ya = y + 1 - 2 * lax.rem(y, 2)
    yb = 3 - y
    yo = 3 - ya
    pair_of = lax.div(seq, 2)
    parity = lax.rem(seq, 2)

    def at(seq_to, dp_to):
        return {"seq": seq_to, "dp": dp_to}

    right = at(lax.rem(seq + 1, N_SEQ), dp)
    left = at(lax.rem(seq + N_SEQ - 1, N_SEQ), dp)
    twin = at(seq, 2 * y + 1 - core)
    at_ya = at(seq, 2 * ya + core)
    at_yb = at(seq, 2 * yb + core)
    fours = []
    for side in (0, 1):
        block = lax.rem(pair_of + (N_SEQ // 2 - 1 if side == 0 else 1), N_SEQ // 2)
        for part in (0, 1):
            fours.append(at(2 * block + part, dp))

    def remote(src, dst, send, recv, device_id):
        return pltpu.make_async_remote_copy(
            src_ref=src, dst_ref=dst, send_sem=send, recv_sem=recv, device_id=device_id, device_id_type=MESH
        )

    load_k = pltpu.make_async_copy(k_hbm, kv.at[0, 0:ROWS], in_sem.at[0])
    load_v = pltpu.make_async_copy(v_hbm, kv.at[1, 0:ROWS], in_sem.at[1])
    load_d = pltpu.make_async_copy(d_hbm, d, in_sem.at[2])
    load_w = pltpu.make_async_copy(w_hbm, w, in_sem.at[3])
    load_q = pltpu.make_async_copy(q_hbm, q, in_sem.at[4])
    for load in (load_k, load_v, load_d, load_w, load_q):
        load.start()
    barrier = pltpu.get_barrier_semaphore()
    partners = [right, left, twin, at_ya, at_yb] + fours
    for partner in partners:
        pl.semaphore_signal(barrier, inc=1, device_id=partner, device_id_type=MESH)

    def greet(number, carry):
        pl.semaphore_signal(barrier, inc=1, device_id=at(lax.rem(seq + number, N_SEQ), dp), device_id_type=MESH)
        return carry

    lax.fori_loop(1, N_SEQ, greet, 0)

    matrix, scale = pool_matrix()
    pooled = []
    for part, load in ((0, load_k), (1, load_v)):
        load.wait()
        sums = dot_nn(matrix, kv[part, 0:ROWS, :]) * scale
        kv[part, OWN1:LEFT, :] = sums[0:96].astype(BF16)
        rim[0, 16 * part : 16 * part + 16] = kv[part, 0:16, :]
        rim[1, 16 * part : 16 * part + 16] = kv[part, 112:128, :]
        pooled.append(sums)

    def of_both(row):
        return jnp.concatenate([sums[row : row + 8] for sums in pooled], axis=0).astype(BF16)

    for side, rows in ((0, (8, 72, 104)), (1, (48, 80, 96))):
        for number, row in enumerate(rows):
            rim[side, 32 + 16 * number : 48 + 16 * number] = of_both(row)
    four[...] = of_both(112)

    pl.semaphore_wait(barrier, len(partners) + N_SEQ - 1)

    def part_of(z_at, step):
        return lax.rem(lax.div(z_at, 2) + 2 - step + 3 * lax.div(step, 2) - 2 * lax.div(step, 3), STEPS)

    def lanes_at(z_at, step):
        return pl.ds(pl.multiple_of(part_of(z_at, step) * WIDE, WIDE), WIDE)

    def lanes_of(step):
        return lanes_at(z, step)

    def pair_lanes(step, pair):
        return pl.ds(pl.multiple_of(part_of(z, step) * WIDE + pair * PAIR, PAIR), PAIR)

    def rim_copies(step, lanes_to):
        copies = []
        for side, partner in ((0, left), (1, right)):
            lanes = lanes_to(partner, step)
            copies.append(
                remote(
                    rim.at[side, :, lanes],
                    rim_in.at[1 - side, :, lanes],
                    rim_s.at[side],
                    rim_r.at[side * STEPS + step],
                    partner,
                )
            )
        return copies

    def four_copies(step, lanes_to):
        copies = []
        for number, partner in enumerate(fours):
            slot = parity + (2 if number < 2 else 0)
            lanes = lanes_to(partner, step)
            copies.append(
                remote(
                    four.at[:, lanes],
                    four_in.at[slot, :, lanes],
                    four_s.at[number],
                    four_r.at[slot * STEPS + step],
                    partner,
                )
            )
        return copies

    for step in range(STEPS):
        for copies in (four_copies, rim_copies):
            for copy in copies(step, lambda partner, step: lanes_at(lax.div(partner["seq"], X), step)):
                copy.start()

    def wait_rims(step):
        lanes = lanes_of(step)
        for copy in rim_copies(step, lambda partner, step: lanes):
            copy.wait_recv()
        for side, row in ((0, LEFT), (1, RIGHT)):
            rows = dot_nn(unfold[side], rim_in[side, :, lanes]) * rim_scale(side)
            kv[0, row : row + 64, lanes] = rows[0:64].astype(BF16)
            kv[1, row : row + 64, lanes] = rows[64:128].astype(BF16)
        for number in range(4):
            remote(
                four.at[:, lanes],
                four_in.at[number, :, lanes],
                four_s.at[number],
                four_r.at[number * STEPS + step],
                fours[number],
            ).wait_recv()
        for side, row in ((0, LEFT4), (1, RIGHT4)):
            one = four_in[2 * side, :, lanes].astype(F32)
            two = four_in[2 * side + 1, :, lanes].astype(F32)
            for part in (0, 1):
                kv[part, row : row + 16, lanes] = jnp.concatenate(
                    [one[8 * part : 8 * part + 8], two[8 * part : 8 * part + 8]], axis=0
                ).astype(BF16)

    load_d.wait()
    mine_rows = pl.ds(pl.multiple_of(core * ROWS, ROWS), ROWS)
    twin_columns = []
    for number, y_to in enumerate((y, ya, yb, yo)):
        columns = slice(number * PAIR, (number + 1) * PAIR)
        theirs = pl.ds(pl.multiple_of(y_to * 256 + (1 - core) * PAIR, PAIR), PAIR)
        copy = remote(
            d.at[:, theirs], pairs_d.at[mine_rows, columns], d2_s.at[number], d2_r.at[number], twin
        )
        copy.start()
        twin_columns.append(copy)

    fill_bias(bias, seq)
    spread[...] = spread_matrix()
    for side in (0, 1):
        unfold[side] = rim_matrix((ROWS, SENT), 0, side)
        fold[side] = rim_matrix((SENT, ROWS), 1, side)
    for part in (0, 1):
        spread_back[part] = jnp.concatenate(spread_sent(part), axis=1).astype(BF16)
    for number, y_to in enumerate((y, ya, yb, yo)):
        ours = pl.ds(pl.multiple_of(y_to * 256 + core * PAIR, PAIR), PAIR)
        pairs_d[mine_rows, number * PAIR : (number + 1) * PAIR] = d[:, ours]
    load_w.wait()
    for column in range(0, WIDTH, 256):
        g[:, column : column + 256] = dot_nt(d[...], w[column : column + 256, :]).astype(BF16)
    load_q.wait()

    for copy in twin_columns:
        copy.wait_recv()

    mine_lanes = pl.ds(pl.multiple_of(core * ROWS, ROWS), ROWS)

    def copy_a(step):
        block = pairs_a.at[step, :, mine_lanes]
        return remote(block, block, a_s.at[step], a_r.at[step], twin)

    def copies_y1(step):
        return (
            remote(y1_out.at[step, 0], y1_in.at[step, 0], y1_s.at[2 * step], y1_r.at[2 * step], at_ya),
            remote(y1_out.at[step, 1], y1_in.at[step, 1], y1_s.at[2 * step + 1], y1_r.at[2 * step + 1], at_yb),
        )

    def copies_y2(step):
        return (
            remote(y2_out.at[step, 0], y2_in.at[step, 0], y2_s.at[2 * step], y2_r.at[2 * step], at_yb),
            remote(y2_out.at[step, 1], y2_in.at[step, 1], y2_s.at[2 * step + 1], y2_r.at[2 * step + 1], at_ya),
        )

    odd_z = lax.rem(z, 2)

    def send_z(step, pair):
        z_to = 2 * part_of(z, step) + pair
        last = lax.div(step, STEPS - 1)
        same = last * (odd_z if pair else 1 - odd_z)

        def copy(apart):
            x_to = lax.rem(x + apart, X)
            rows = pl.ds(pl.multiple_of(pair * PAIR + x_to * 32, 32), 32)
            slot = 8 * step + (1 - last) * 4 * odd_z + 3 * same + apart
            return remote(
                z_out.at[step, rows], z_in.at[slot], z_s.at[0], z_r.at[0], at(z_to * X + x_to, dp)
            )

        @pl.when(same == 0)
        def _():
            copy(0).start()

        for apart in range(1, X):
            copy(apart).start()

    def forward(step):
        lanes = [pair_lanes(step, pair) for pair in (0, 1)]
        query_rows = [two_heads(q[:, at_lanes], 0.125) for at_lanes in lanes]
        scores = [dot_nt(kv[0, :, at_lanes], rows) + bias[...] for at_lanes, rows in zip(lanes, query_rows)]
        tops = [jnp.max(score, axis=0, keepdims=True) for score in scores]
        exponents = [jnp.exp(score - top) for score, top in zip(scores, tops)]
        shares = [1.0 / jnp.sum(exponent, axis=0, keepdims=True) for exponent in exponents]
        normal = [exponent * share for exponent, share in zip(exponents, shares)]
        halves = [weight.astype(BF16) for weight in normal]
        attended = [
            one_of_two(dot_tn(kv[1, :, at_lanes], half)).astype(BF16) for at_lanes, half in zip(lanes, halves)
        ]
        for pair in (0, 1):
            weights[2 * step + pair] = normal[pair]
            weights_half[2 * step + pair] = halves[pair]
            pairs_a[step, pair * PAIR : (pair + 1) * PAIR, mine_lanes] = attended[pair]
        copy_a(step).start()

    def project(step):
        copy_a(step).wait_recv()
        partial = dot_nn(pairs_a[step], pairs_d[...])
        kept[step] = partial[:, 0:128]
        kept2[step, 0:128] = partial[0:128, 256:384]
        kept2[step, 128:256] = partial[128:256, 128:256]
        y1_out[step, 0, 0:128] = partial[0:128, 128:256].astype(BF16)
        y1_out[step, 0, 128:256] = partial[0:128, 384:512].astype(BF16)
        y1_out[step, 1, 0:128] = partial[128:256, 256:384].astype(BF16)
        y1_out[step, 1, 128:256] = partial[128:256, 384:512].astype(BF16)
        for copy in copies_y1(step):
            copy.start()

    def fold_y1(step):
        for copy in copies_y1(step):
            copy.wait_recv()
        for half in (0, 1):
            rows = slice(128 * half, 128 * half + 128)
            kept[step, rows] = kept[step, rows] + y1_in[step, half, 0:128].astype(F32)
            y2_out[step, half] = (kept2[step, rows] + y1_in[step, half, 128:256].astype(F32)).astype(BF16)
        for copy in copies_y2(step):
            copy.start()

    def fold_y2(step):
        for copy in copies_y2(step):
            copy.wait_recv()
        for half in (0, 1):
            rows = slice(128 * half, 128 * half + 128)
            total = kept[step, rows] + y2_in[step, half].astype(F32)
            kept[step, rows] = total
            z_out[step, rows] = total.astype(BF16)
        for pair in (0, 1):
            send_z(step, pair)

    def backward_rims(step):
        steps = (2 * step, 2 * step + 1)
        lanes = [pair_lanes(step, pair) for pair in (0, 1)]
        query_rows = [two_heads(q[:, at_lanes], 0.125) for at_lanes in lanes]
        grad_rows = [two_heads(g[:, at_lanes], 1.0) for at_lanes in lanes]
        d_probs = [dot_nt(kv[1, :, at_lanes], rows) for at_lanes, rows in zip(lanes, grad_rows)]
        normal = [weights[number] for number in steps]
        own_scale = level_scale(lax.rem(lax.broadcasted_iota(jnp.int32, (ROWS, 1), 0), 64) // 16)
        deltas = [jnp.sum(weight * d_prob, axis=0, keepdims=True) for weight, d_prob in zip(normal, d_probs)]
        d_scores = [
            (weight * (d_prob - delta)).astype(BF16) for weight, d_prob, delta in zip(normal, d_probs, deltas)
        ]
        d_keys = [dot_nn(d_score[LEFT:], rows) for d_score, rows in zip(d_scores, query_rows)]
        d_values = [dot_nn(weights_half[number, LEFT:, :], rows) for number, rows in zip(steps, grad_rows)]
        for number, at_lanes, d_score, d_key, d_value in zip(steps, lanes, d_scores, d_keys, d_values):
            grad_scores[number] = d_score
            for side in (0, 1):
                rows = slice(64 * side, 64 * side + 64)
                grads = jnp.concatenate([d_key[rows], d_value[rows]], axis=0) * own_scale
                back_rim[side, :, at_lanes] = dot_nn(fold[side], grads.astype(BF16)).astype(BF16)
            for number in range(4):
                rows = slice(128 + 8 * number, 136 + 8 * number)
                both = jnp.concatenate([d_key[rows], d_value[rows]], axis=0) * 0.25
                back_four[number, :, at_lanes] = both.astype(BF16)
        for at_lanes in [lanes_of(step)]:
            remote(
                back_rim.at[0, :, at_lanes], back_in.at[0:SENT, at_lanes], back_s.at[0], back_r.at[0], left
            ).start()
            remote(
                back_rim.at[1, :, at_lanes], back_in.at[SENT : 2 * SENT, at_lanes], back_s.at[1], back_r.at[1], right
            ).start()
            for number, partner in enumerate(fours):
                slot = parity + (2 if number < 2 else 0)
                remote(
                    back_four.at[number, :, at_lanes],
                    back_four_in.at[slot, :, at_lanes],
                    bfour_s.at[number],
                    bfour_r.at[slot],
                    partner,
                ).start()

    def backward_own(step):
        steps = (2 * step, 2 * step + 1)
        lanes = [pair_lanes(step, pair) for pair in (0, 1)]
        query_rows = [two_heads(q[:, at_lanes], 0.125) for at_lanes in lanes]
        grad_rows = [two_heads(g[:, at_lanes], 1.0) for at_lanes in lanes]
        d_queries = [
            one_of_two(dot_tn(kv[0, :, at_lanes], grad_scores[number])) * 0.125 for number, at_lanes in zip(steps, lanes)
        ]
        d_keys = [dot_nn(grad_scores[number, 0:LEFT, :], rows) for number, rows in zip(steps, query_rows)]
        d_values = [dot_nn(weights_half[number, 0:LEFT, :], rows) for number, rows in zip(steps, grad_rows)]
        for at_lanes, d_query, d_key, d_value in zip(lanes, d_queries, d_keys, d_values):
            dq_ref[:, at_lanes] = d_query.T.astype(BF16)
            for part, grad in ((0, d_key), (1, d_value)):
                own[part, :, at_lanes] = grad[0:ROWS]
                back[part, 0:64, at_lanes] = (grad[OWN1:OWN2] * 2.0 ** (-0.5)).astype(BF16)
                back[part, 64:96, at_lanes] = (grad[OWN2:LEFT] * 0.5).astype(BF16)

    def forward_step(step, carry):
        wait_rims(step)
        forward(step)

        @pl.when(step >= 1)
        def _():
            project(step - 1)

        return carry

    def rims_step(step, carry):
        backward_rims(step)

        @pl.when(step == 0)
        def _():
            project(step + 3)

        @pl.when(lax.rem(step, 2) == 1)
        def _():
            fold_y1(step // 2)

        return carry

    def own_step(step, carry):
        backward_own(step)

        @pl.when(lax.rem(step, 2) == 1)
        def _():
            fold_y2(step // 2)
            fold_y1(2 + step // 2)

        return carry

    lax.fori_loop(0, STEPS, forward_step, 0)
    lax.fori_loop(0, STEPS, rims_step, 0)
    lax.fori_loop(0, STEPS, own_step, 0)
    for step in (2, 3):
        fold_y2(step)
    store_q = pltpu.make_async_copy(dq_ref, dq_hbm, out_sem.at[0])
    store_q.start()

    rim_left = remote(back_rim.at[0], back_in.at[0:SENT], back_s.at[0], back_r.at[0], left)
    rim_right = remote(back_rim.at[1], back_in.at[SENT : 2 * SENT], back_s.at[1], back_r.at[1], right)
    rim_left.wait_recv()
    rim_right.wait_recv()
    for number in range(4):
        remote(
            back_four.at[number], back_four_in.at[number], bfour_s.at[number], bfour_r.at[number], fours[number]
        ).wait_recv()
    stores = [store_q]
    for part, out in ((0, dk_ref), (1, dv_ref)):
        for column in range(0, WIDTH, 256):
            columns = slice(column, column + 256)
            rows4 = [back_four_in[number, :, columns].astype(F32)[8 * part : 8 * part + 8] for number in range(4)]
            back[part, 96:128, columns] = jnp.concatenate(rows4, axis=0).astype(BF16)
            total = own[part, :, columns] + dot_nn(spread[...], back[part, :, columns])
            out[:, columns] = (total + dot_nn(spread_back[part], back_in[:, columns])).astype(BF16)
        store = pltpu.make_async_copy(out, (dk_hbm, dv_hbm)[part], out_sem.at[1 + part])
        store.start()
        stores.append(store)

    all_z = remote(z_in, z_in, z_s.at[0], z_r.at[0], right)
    all_z.wait_recv()
    mine = kept[STEPS - 1, pl.ds(pl.multiple_of(odd_z * PAIR + x * 32, 32), 32), :]
    gw_ref[...] = (mine + jnp.sum(z_in[...].astype(F32), axis=0)) * FACTOR
    store = pltpu.make_async_copy(gw_ref, gw_hbm, out_sem.at[3])
    store.start()
    stores.append(store)

    sent_rims = [
        remote(rim.at[side], rim_in.at[side], rim_s.at[side], rim_r.at[0], right) for side in (0, 1)
    ]
    sent_four = [
        remote(four, four_in.at[number], four_s.at[number], four_r.at[number], fours[number]) for number in range(4)
    ]
    for copy in sent_rims + sent_four + twin_columns + [rim_left, rim_right, all_z]:
        copy.wait_send()
    for number in range(4):
        remote(
            back_four.at[number], back_four_in.at[number], bfour_s.at[number], bfour_r.at[number], fours[number]
        ).wait_send()

    def wait_sends(step, carry):
        copy_a(step).wait_send()
        for copy in copies_y1(step) + copies_y2(step):
            copy.wait_send()
        return carry

    lax.fori_loop(0, STEPS, wait_sends, 0)
    for store in stores:
        store.wait()


def hand_on(*refs):
    given, results, held, sems = refs[0:4], refs[4:8], refs[8:12], refs[12]
    loads = [pltpu.make_async_copy(given[i], held[i], sems.at[i]) for i in range(4)]
    stores = [pltpu.make_async_copy(held[i], results[i], sems.at[4 + i]) for i in range(4)]
    for load in loads:
        load.start()
    for load, store in zip(loads, stores):
        load.wait()
        store.start()
    for store in stores:
        store.wait()


def on_device(queries, keys, values, d_out, w_out):
    dma = pltpu.SemaphoreType.DMA
    any_space = pl.BlockSpec(memory_space=pl.ANY)
    rows_shape = jax.ShapeDtypeStruct((ROWS, WIDTH), BF16)
    grad_shape = jax.ShapeDtypeStruct((32, 128), F32)
    results = (rows_shape, rows_shape, rows_shape, grad_shape)
    held = [pltpu.VMEM(result.shape, result.dtype) for result in results]
    outs = pl.pallas_call(
        kernel,
        out_shape=results,
        in_specs=[any_space] * 5,
        out_specs=(any_space,) * 4,
        scratch_shapes=held
        + [
            pltpu.VMEM((ROWS, WIDTH), BF16),
            pltpu.VMEM((ROWS, WIDTH), BF16),
            pltpu.VMEM((WIDTH, WIDTH), BF16),
            pltpu.VMEM((ROWS, WIDTH), BF16),
            pltpu.VMEM((2, KEYS, WIDTH), BF16),
            pltpu.VMEM((KEYS, 2 * ROWS), F32),
            pltpu.VMEM((ROWS, ROWS), BF16),
            pltpu.VMEM((2, ROWS, 2 * SENT), BF16),
            pltpu.VMEM((2, ROWS, SENT), BF16),
            pltpu.VMEM((2, SENT, ROWS), BF16),
            pltpu.VMEM((2, SENT, WIDTH), BF16),
            pltpu.VMEM((2, SENT, WIDTH), BF16),
            pltpu.VMEM((16, WIDTH), BF16),
            pltpu.VMEM((4, 16, WIDTH), BF16),
            pltpu.VMEM((PAIRS, KEYS, 2 * ROWS), F32),
            pltpu.VMEM((PAIRS, KEYS, 2 * ROWS), BF16),
            pltpu.VMEM((PAIRS, KEYS, 2 * ROWS), BF16),
            pltpu.VMEM((2, ROWS, WIDTH), F32),
            pltpu.VMEM((2, ROWS, WIDTH), BF16),
            pltpu.VMEM((2 * SENT, WIDTH), BF16),
            pltpu.VMEM((2, SENT, WIDTH), BF16),
            pltpu.VMEM((4, 16, WIDTH), BF16),
            pltpu.VMEM((4, 16, WIDTH), BF16),
            pltpu.VMEM((STEPS, WIDE, 2 * ROWS), BF16),
            pltpu.VMEM((2 * ROWS, 512), BF16),
            pltpu.VMEM((STEPS, WIDE, 128), F32),
            pltpu.VMEM((STEPS, WIDE, 128), F32),
            pltpu.VMEM((STEPS, 2, WIDE, 128), BF16),
            pltpu.VMEM((STEPS, 2, WIDE, 128), BF16),
            pltpu.VMEM((STEPS, 2, 128, 128), BF16),
            pltpu.VMEM((STEPS, 2, 128, 128), BF16),
            pltpu.VMEM((STEPS, WIDE, 128), BF16),
            pltpu.VMEM((N_SEQ - 1, 32, 128), BF16),
            dma((5,)),
            dma((4,)),
            dma((2,)), dma((2 * STEPS,)),
            dma((4,)), dma((4 * STEPS,)),
            dma((4,)), dma((4,)),
            dma((STEPS,)), dma((STEPS,)),
            dma((2 * STEPS,)), dma((2 * STEPS,)),
            dma((2 * STEPS,)), dma((2 * STEPS,)),
            dma((1,)), dma((1,)),
            dma((2,)), dma((2,)),
            dma((4,)), dma((4,)),
        ],
        compiler_params=pltpu.CompilerParams(
            collective_id=0, has_side_effects=True, vmem_limit_bytes=VMEM_BYTES
        ),
    )(queries[0], keys[0], values[0], d_out[0], w_out)
    d_queries, d_keys, d_values, grad_w = pl.pallas_call(
        hand_on,
        out_shape=results,
        in_specs=[any_space] * 4,
        out_specs=(any_space,) * 4,
        scratch_shapes=held + [dma((8,))],
        compiler_params=pltpu.CompilerParams(vmem_limit_bytes=VMEM_BYTES),
    )(*outs)
    return d_queries[None], d_keys[None], d_values[None], grad_w


def solution(mesh):
    placed = P("dp", "seq", None)
    return jax.shard_map(
        on_device,
        mesh=mesh,
        in_specs=(placed, placed, placed, placed, P()),
        out_specs=(placed, placed, placed, P("seq", "dp")),
        check_vma=False,
    )
```

```python
import jax
import jax.numpy as jnp
from jax import lax
from jax.experimental import pallas as pl
from jax.experimental.pallas import tpu as pltpu
from jax.sharding import PartitionSpec as P

ROWS = 128
WIDTH = 1024
PAIR = 128
PAIRS = 8
KEYS = 384
N_SEQ = 32
X, Z = 4, 8
FACTOR = 32768 ** (-0.5)
STEPS = 4
SENT = 80
WIDE = 256
VMEM_BYTES = 56 * 1024 * 1024
MESH = pl.DeviceIdType.MESH
F32 = jnp.float32
BF16 = jnp.bfloat16

OWN1, OWN2, LEFT, RIGHT, LEFT4, RIGHT4 = 128, 192, 224, 288, 352, 368


def dot_nt(a, b):
    return lax.dot_general(a, b, (((1,), (1,)), ((), ())), preferred_element_type=F32)


def dot_tn(a, b):
    return lax.dot_general(a, b, (((0,), (0,)), ((), ())), preferred_element_type=F32)


def dot_nn(a, b):
    return lax.dot_general(a, b, (((1,), (0,)), ((), ())), preferred_element_type=F32)


def two_heads(block, scale):
    lane = lax.broadcasted_iota(jnp.int32, (1, PAIR), 1)
    first = jnp.where(lane < 64, scale, 0.0).astype(BF16)
    second = jnp.where(lane < 64, 0.0, scale).astype(BF16)
    return jnp.concatenate([block * first, block * second], axis=0)


def one_of_two(both):
    row = lax.broadcasted_iota(jnp.int32, (PAIR, ROWS), 0)
    return jnp.where(row < 64, both[:, :ROWS], both[:, ROWS:])


def pool_matrix():
    row = lax.broadcasted_iota(jnp.int32, (ROWS, ROWS), 0)
    token = lax.broadcasted_iota(jnp.int32, (ROWS, ROWS), 1)
    level = jnp.where(row < 64, 1, jnp.where(row < 96, 2, jnp.where(row < 112, 3, 4)))
    base = jnp.where(row < 64, 0, jnp.where(row < 96, 64, jnp.where(row < 112, 96, 112)))
    matrix = jnp.where(lax.shift_right_logical(token, level) == row - base, 1.0, 0.0).astype(BF16)
    row = lax.broadcasted_iota(jnp.int32, (ROWS, 1), 0)
    scale = jnp.where(
        row < 64, 2.0 ** (-0.5), jnp.where(row < 96, 0.5, jnp.where(row < 112, 2.0 ** (-1.5), 0.25))
    ).astype(F32)
    return matrix, scale


def rim_row(row, side):
    level = lax.rem(row, 64) // 16
    within = lax.rem(row, 16)
    if side == 0:
        within = within + jnp.where(level == 0, 112, jnp.where(level == 1, 48, jnp.where(level == 2, 16, 0)))
    return row // 64, level, within


def sent_row(row, side):
    fine = row < 32
    level = jnp.where(fine, 0, (row - 16) // 16)
    part = jnp.where(fine, row // 16, lax.rem(row, 16) // 8)
    within = jnp.where(fine, lax.rem(row, 16), lax.rem(row, 8))
    if side == 0:
        base = jnp.where(fine, 112, jnp.where(level == 1, 48, jnp.where(level == 2, 16, 0)))
    else:
        base = jnp.where(fine, 0, 8)
    return part, level, lax.shift_left(base + within, level)


def rim_matrix(shape, rim_axis, side):
    part, level, position = rim_row(lax.broadcasted_iota(jnp.int32, shape, rim_axis), side)
    from_part, _, first = sent_row(lax.broadcasted_iota(jnp.int32, shape, 1 - rim_axis), side)
    covered = (part == from_part) & (lax.shift_right_logical(first, level) == position)
    return jnp.where(covered, 1.0, 0.0).astype(BF16)


def level_scale(level):
    return jnp.where(
        level == 0, 1.0, jnp.where(level == 1, 2.0 ** (-0.5), jnp.where(level == 2, 0.5, 2.0 ** (-1.5)))
    ).astype(F32)


def rim_scale(side):
    _, level, position = rim_row(lax.broadcasted_iota(jnp.int32, (ROWS, 1), 0), side)
    token = lax.shift_left(position, level)
    if side == 0:
        source = jnp.where(token >= 112, 0, jnp.where(token >= 96, 1, jnp.where(token >= 64, 2, 3)))
    else:
        source = jnp.where(token < 16, 0, jnp.where(token < 32, 1, jnp.where(token < 64, 2, 3)))
    return level_scale(level - source)


def spread_matrix():
    token = lax.broadcasted_iota(jnp.int32, (ROWS, ROWS), 0)
    row = lax.broadcasted_iota(jnp.int32, (ROWS, ROWS), 1)
    level = jnp.where(row < 64, 1, jnp.where(row < 96, 2, 4))
    target = jnp.where(row < 64, row, jnp.where(row < 96, row - 64, lax.rem(row - 96, 8)))
    return jnp.where(lax.shift_right_logical(token, level) == target, 1.0, 0.0).astype(BF16)


def spread_sent(part):
    columns = []
    for side in (0, 1):
        token = lax.broadcasted_iota(jnp.int32, (ROWS, SENT), 0)
        of_part, level, first = sent_row(lax.broadcasted_iota(jnp.int32, (ROWS, SENT), 1), side)
        same = lax.shift_right_logical(token, level) == lax.shift_right_logical(first, level)
        columns.append(jnp.where((of_part == part) & same, 1.0, 0.0))
    return columns


def fill_bias(bias, device):
    token = lax.rem(lax.broadcasted_iota(jnp.int32, (16, 2 * ROWS), 1), ROWS)
    not_first = device > 0
    not_last = device < N_SEQ - 1

    def put(row, valid):
        bias[row : row + 16, :] = jnp.where(valid, 0.0, -1e30).astype(F32)

    for block in range(8):
        near = token // 16 - block
        put(16 * block, (near >= -1) & (near <= 1))
    for block in range(4):
        near = token // 32 - block
        put(OWN1 + 16 * block, (near == -1) | (near == 1))
    for block in range(2):
        put(OWN2 + 16 * block, token // 64 != block)
    for level in range(4):
        span = 16 * 2**level
        put(LEFT + 16 * level, (token < span) & not_first)
        put(RIGHT + 16 * level, (token >= ROWS - span) & not_last)
    always = token >= 0
    put(LEFT4, always & (device >= 2))
    put(RIGHT4, always & (device < N_SEQ - 2))


def kernel(
    q_hbm, k_hbm, v_hbm, d_hbm, w_hbm,
    dq_ref, dk_ref, dv_ref, gw_ref, q, d, w, g, kv, bias, spread, spread_back, unfold, fold,
    rim, rim_in, four, four_in,
    weights, weights_half, grad_scores, own, back, back_in, back_rim, back_four, back_four_in,
    pairs_a, pairs_d, kept, kept2, y1_out, y1_in, y2_out, y2_in, z_out, z_in,
    in_sem, rim_s, rim_r, four_s, four_r, d2_s, d2_r, a_s, a_r, y1_s, y1_r, y2_s, y2_r,
    z_s, z_r, back_s, back_r, bfour_s, bfour_r,
):
    seq = lax.axis_index("seq")
    dp = lax.axis_index("dp")
    z, x = lax.div(seq, X), lax.rem(seq, X)
    y, core = lax.div(dp, 2), lax.rem(dp, 2)
    ya = y + 1 - 2 * lax.rem(y, 2)
    yb = 3 - y
    yo = 3 - ya
    pair_of = lax.div(seq, 2)
    parity = lax.rem(seq, 2)

    def at(seq_to, dp_to):
        return {"seq": seq_to, "dp": dp_to}

    right = at(lax.rem(seq + 1, N_SEQ), dp)
    left = at(lax.rem(seq + N_SEQ - 1, N_SEQ), dp)
    twin = at(seq, 2 * y + 1 - core)
    at_ya = at(seq, 2 * ya + core)
    at_yb = at(seq, 2 * yb + core)
    fours = []
    for side in (0, 1):
        block = lax.rem(pair_of + (N_SEQ // 2 - 1 if side == 0 else 1), N_SEQ // 2)
        for part in (0, 1):
            fours.append(at(2 * block + part, dp))

    def remote(src, dst, send, recv, device_id):
        return pltpu.make_async_remote_copy(
            src_ref=src, dst_ref=dst, send_sem=send, recv_sem=recv, device_id=device_id, device_id_type=MESH
        )

    load_k = pltpu.make_async_copy(k_hbm, kv.at[0, 0:ROWS], in_sem.at[0])
    load_v = pltpu.make_async_copy(v_hbm, kv.at[1, 0:ROWS], in_sem.at[1])
    load_d = pltpu.make_async_copy(d_hbm, d, in_sem.at[2])
    load_w = pltpu.make_async_copy(w_hbm, w, in_sem.at[3])
    load_q = pltpu.make_async_copy(q_hbm, q, in_sem.at[4])
    for load in (load_k, load_v, load_d, load_w, load_q):
        load.start()
    barrier = pltpu.get_barrier_semaphore()
    partners = [right, left, twin, at_ya, at_yb] + fours
    for partner in partners:
        pl.semaphore_signal(barrier, inc=1, device_id=partner, device_id_type=MESH)

    def greet(number, carry):
        pl.semaphore_signal(barrier, inc=1, device_id=at(lax.rem(seq + number, N_SEQ), dp), device_id_type=MESH)
        return carry

    lax.fori_loop(1, N_SEQ, greet, 0)

    matrix, scale = pool_matrix()
    pooled = []
    for part, load in ((0, load_k), (1, load_v)):
        load.wait()
        sums = dot_nn(matrix, kv[part, 0:ROWS, :]) * scale
        kv[part, OWN1:LEFT, :] = sums[0:96].astype(BF16)
        rim[0, 16 * part : 16 * part + 16] = kv[part, 0:16, :]
        rim[1, 16 * part : 16 * part + 16] = kv[part, 112:128, :]
        pooled.append(sums)

    def of_both(row):
        return jnp.concatenate([sums[row : row + 8] for sums in pooled], axis=0).astype(BF16)

    for side, rows in ((0, (8, 72, 104)), (1, (48, 80, 96))):
        for number, row in enumerate(rows):
            rim[side, 32 + 16 * number : 48 + 16 * number] = of_both(row)
    four[...] = of_both(112)

    pl.semaphore_wait(barrier, len(partners) + N_SEQ - 1)

    def part_of(z_at, step):
        return lax.rem(lax.div(z_at, 2) + 2 - step + 3 * lax.div(step, 2) - 2 * lax.div(step, 3), STEPS)

    def lanes_at(z_at, step):
        return pl.ds(pl.multiple_of(part_of(z_at, step) * WIDE, WIDE), WIDE)

    def lanes_of(step):
        return lanes_at(z, step)

    def pair_lanes(step, pair):
        return pl.ds(pl.multiple_of(part_of(z, step) * WIDE + pair * PAIR, PAIR), PAIR)

    def rim_copies(step, lanes_to):
        copies = []
        for side, partner in ((0, left), (1, right)):
            lanes = lanes_to(partner, step)
            copies.append(
                remote(
                    rim.at[side, :, lanes],
                    rim_in.at[1 - side, :, lanes],
                    rim_s.at[side],
                    rim_r.at[side * STEPS + step],
                    partner,
                )
            )
        return copies

    def four_copies(step, lanes_to):
        copies = []
        for number, partner in enumerate(fours):
            slot = parity + (2 if number < 2 else 0)
            lanes = lanes_to(partner, step)
            copies.append(
                remote(
                    four.at[:, lanes],
                    four_in.at[slot, :, lanes],
                    four_s.at[number],
                    four_r.at[slot * STEPS + step],
                    partner,
                )
            )
        return copies

    for step in range(STEPS):
        for copies in (four_copies, rim_copies):
            for copy in copies(step, lambda partner, step: lanes_at(lax.div(partner["seq"], X), step)):
                copy.start()

    def wait_rims(step):
        lanes = lanes_of(step)
        for copy in rim_copies(step, lambda partner, step: lanes):
            copy.wait_recv()
        for side, row in ((0, LEFT), (1, RIGHT)):
            rows = dot_nn(unfold[side], rim_in[side, :, lanes]) * rim_scale(side)
            kv[0, row : row + 64, lanes] = rows[0:64].astype(BF16)
            kv[1, row : row + 64, lanes] = rows[64:128].astype(BF16)
        for number in range(4):
            remote(
                four.at[:, lanes],
                four_in.at[number, :, lanes],
                four_s.at[number],
                four_r.at[number * STEPS + step],
                fours[number],
            ).wait_recv()
        for side, row in ((0, LEFT4), (1, RIGHT4)):
            one = four_in[2 * side, :, lanes].astype(F32)
            two = four_in[2 * side + 1, :, lanes].astype(F32)
            for part in (0, 1):
                kv[part, row : row + 16, lanes] = jnp.concatenate(
                    [one[8 * part : 8 * part + 8], two[8 * part : 8 * part + 8]], axis=0
                ).astype(BF16)

    load_d.wait()
    mine_rows = pl.ds(pl.multiple_of(core * ROWS, ROWS), ROWS)
    twin_columns = []
    for number, y_to in enumerate((y, ya, yb, yo)):
        columns = slice(number * PAIR, (number + 1) * PAIR)
        theirs = pl.ds(pl.multiple_of(y_to * 256 + (1 - core) * PAIR, PAIR), PAIR)
        copy = remote(
            d.at[:, theirs], pairs_d.at[mine_rows, columns], d2_s.at[number], d2_r.at[number], twin
        )
        copy.start()
        twin_columns.append(copy)

    fill_bias(bias, seq)
    spread[...] = spread_matrix()
    for side in (0, 1):
        unfold[side] = rim_matrix((ROWS, SENT), 0, side)
        fold[side] = rim_matrix((SENT, ROWS), 1, side)
    for part in (0, 1):
        spread_back[part] = jnp.concatenate(spread_sent(part), axis=1).astype(BF16)
    for number, y_to in enumerate((y, ya, yb, yo)):
        ours = pl.ds(pl.multiple_of(y_to * 256 + core * PAIR, PAIR), PAIR)
        pairs_d[mine_rows, number * PAIR : (number + 1) * PAIR] = d[:, ours]
    load_w.wait()
    for column in range(0, WIDTH, 256):
        g[:, column : column + 256] = dot_nt(d[...], w[column : column + 256, :]).astype(BF16)
    load_q.wait()

    for copy in twin_columns:
        copy.wait_recv()

    mine_lanes = pl.ds(pl.multiple_of(core * ROWS, ROWS), ROWS)

    def copy_a(step):
        block = pairs_a.at[step, :, mine_lanes]
        return remote(block, block, a_s.at[step], a_r.at[step], twin)

    def copies_y1(step):
        return (
            remote(y1_out.at[step, 0], y1_in.at[step, 0], y1_s.at[2 * step], y1_r.at[2 * step], at_ya),
            remote(y1_out.at[step, 1], y1_in.at[step, 1], y1_s.at[2 * step + 1], y1_r.at[2 * step + 1], at_yb),
        )

    def copies_y2(step):
        return (
            remote(y2_out.at[step, 0], y2_in.at[step, 0], y2_s.at[2 * step], y2_r.at[2 * step], at_yb),
            remote(y2_out.at[step, 1], y2_in.at[step, 1], y2_s.at[2 * step + 1], y2_r.at[2 * step + 1], at_ya),
        )

    odd_z = lax.rem(z, 2)

    def send_z(step, pair):
        z_to = 2 * part_of(z, step) + pair
        last = lax.div(step, STEPS - 1)
        same = last * (odd_z if pair else 1 - odd_z)

        def copy(apart):
            x_to = lax.rem(x + apart, X)
            rows = pl.ds(pl.multiple_of(pair * PAIR + x_to * 32, 32), 32)
            slot = 8 * step + (1 - last) * 4 * odd_z + 3 * same + apart
            return remote(
                z_out.at[step, rows], z_in.at[slot], z_s.at[0], z_r.at[0], at(z_to * X + x_to, dp)
            )

        @pl.when(same == 0)
        def _():
            copy(0).start()

        for apart in range(1, X):
            copy(apart).start()

    def forward(step):
        lanes = [pair_lanes(step, pair) for pair in (0, 1)]
        query_rows = [two_heads(q[:, at_lanes], 0.125) for at_lanes in lanes]
        scores = [dot_nt(kv[0, :, at_lanes], rows) + bias[...] for at_lanes, rows in zip(lanes, query_rows)]
        tops = [jnp.max(score, axis=0, keepdims=True) for score in scores]
        exponents = [jnp.exp(score - top) for score, top in zip(scores, tops)]
        shares = [1.0 / jnp.sum(exponent, axis=0, keepdims=True) for exponent in exponents]
        normal = [exponent * share for exponent, share in zip(exponents, shares)]
        halves = [weight.astype(BF16) for weight in normal]
        attended = [
            one_of_two(dot_tn(kv[1, :, at_lanes], half)).astype(BF16) for at_lanes, half in zip(lanes, halves)
        ]
        for pair in (0, 1):
            weights[2 * step + pair] = normal[pair]
            weights_half[2 * step + pair] = halves[pair]
            pairs_a[step, pair * PAIR : (pair + 1) * PAIR, mine_lanes] = attended[pair]
        copy_a(step).start()

    def project(step):
        copy_a(step).wait_recv()
        partial = dot_nn(pairs_a[step], pairs_d[...])
        kept[step] = partial[:, 0:128]
        kept2[step, 0:128] = partial[0:128, 256:384]
        kept2[step, 128:256] = partial[128:256, 128:256]
        y1_out[step, 0, 0:128] = partial[0:128, 128:256].astype(BF16)
        y1_out[step, 0, 128:256] = partial[0:128, 384:512].astype(BF16)
        y1_out[step, 1, 0:128] = partial[128:256, 256:384].astype(BF16)
        y1_out[step, 1, 128:256] = partial[128:256, 384:512].astype(BF16)
        for copy in copies_y1(step):
            copy.start()

    def fold_y1(step):
        for copy in copies_y1(step):
            copy.wait_recv()
        for half in (0, 1):
            rows = slice(128 * half, 128 * half + 128)
            kept[step, rows] = kept[step, rows] + y1_in[step, half, 0:128].astype(F32)
            y2_out[step, half] = (kept2[step, rows] + y1_in[step, half, 128:256].astype(F32)).astype(BF16)
        for copy in copies_y2(step):
            copy.start()

    def fold_y2(step):
        for copy in copies_y2(step):
            copy.wait_recv()
        for half in (0, 1):
            rows = slice(128 * half, 128 * half + 128)
            total = kept[step, rows] + y2_in[step, half].astype(F32)
            kept[step, rows] = total
            z_out[step, rows] = total.astype(BF16)
        for pair in (0, 1):
            send_z(step, pair)

    def backward_rims(step):
        steps = (2 * step, 2 * step + 1)
        lanes = [pair_lanes(step, pair) for pair in (0, 1)]
        query_rows = [two_heads(q[:, at_lanes], 0.125) for at_lanes in lanes]
        grad_rows = [two_heads(g[:, at_lanes], 1.0) for at_lanes in lanes]
        d_probs = [dot_nt(kv[1, :, at_lanes], rows) for at_lanes, rows in zip(lanes, grad_rows)]
        normal = [weights[number] for number in steps]
        own_scale = level_scale(lax.rem(lax.broadcasted_iota(jnp.int32, (ROWS, 1), 0), 64) // 16)
        deltas = [jnp.sum(weight * d_prob, axis=0, keepdims=True) for weight, d_prob in zip(normal, d_probs)]
        d_scores = [
            (weight * (d_prob - delta)).astype(BF16) for weight, d_prob, delta in zip(normal, d_probs, deltas)
        ]
        d_keys = [dot_nn(d_score[LEFT:], rows) for d_score, rows in zip(d_scores, query_rows)]
        d_values = [dot_nn(weights_half[number, LEFT:, :], rows) for number, rows in zip(steps, grad_rows)]
        for number, at_lanes, d_score, d_key, d_value in zip(steps, lanes, d_scores, d_keys, d_values):
            grad_scores[number] = d_score
            for side in (0, 1):
                rows = slice(64 * side, 64 * side + 64)
                grads = jnp.concatenate([d_key[rows], d_value[rows]], axis=0) * own_scale
                back_rim[side, :, at_lanes] = dot_nn(fold[side], grads.astype(BF16)).astype(BF16)
            for number in range(4):
                rows = slice(128 + 8 * number, 136 + 8 * number)
                both = jnp.concatenate([d_key[rows], d_value[rows]], axis=0) * 0.25
                back_four[number, :, at_lanes] = both.astype(BF16)
        for at_lanes in [lanes_of(step)]:
            remote(
                back_rim.at[0, :, at_lanes], back_in.at[0:SENT, at_lanes], back_s.at[0], back_r.at[0], left
            ).start()
            remote(
                back_rim.at[1, :, at_lanes], back_in.at[SENT : 2 * SENT, at_lanes], back_s.at[1], back_r.at[1], right
            ).start()
            for number, partner in enumerate(fours):
                slot = parity + (2 if number < 2 else 0)
                remote(
                    back_four.at[number, :, at_lanes],
                    back_four_in.at[slot, :, at_lanes],
                    bfour_s.at[number],
                    bfour_r.at[slot],
                    partner,
                ).start()

    def backward_own(step):
        steps = (2 * step, 2 * step + 1)
        lanes = [pair_lanes(step, pair) for pair in (0, 1)]
        query_rows = [two_heads(q[:, at_lanes], 0.125) for at_lanes in lanes]
        grad_rows = [two_heads(g[:, at_lanes], 1.0) for at_lanes in lanes]
        d_queries = [
            one_of_two(dot_tn(kv[0, :, at_lanes], grad_scores[number])) * 0.125 for number, at_lanes in zip(steps, lanes)
        ]
        d_keys = [dot_nn(grad_scores[number, 0:LEFT, :], rows) for number, rows in zip(steps, query_rows)]
        d_values = [dot_nn(weights_half[number, 0:LEFT, :], rows) for number, rows in zip(steps, grad_rows)]
        for at_lanes, d_query, d_key, d_value in zip(lanes, d_queries, d_keys, d_values):
            dq_ref[:, at_lanes] = d_query.T.astype(BF16)
            for part, grad in ((0, d_key), (1, d_value)):
                own[part, :, at_lanes] = grad[0:ROWS]
                back[part, 0:64, at_lanes] = (grad[OWN1:OWN2] * 2.0 ** (-0.5)).astype(BF16)
                back[part, 64:96, at_lanes] = (grad[OWN2:LEFT] * 0.5).astype(BF16)

    def forward_step(step, carry):
        wait_rims(step)
        forward(step)

        @pl.when(step >= 1)
        def _():
            project(step - 1)

        return carry

    def rims_step(step, carry):
        backward_rims(step)

        @pl.when(step == 0)
        def _():
            project(step + 3)

        @pl.when(lax.rem(step, 2) == 1)
        def _():
            fold_y1(step // 2)

        return carry

    def own_step(step, carry):
        backward_own(step)

        @pl.when(lax.rem(step, 2) == 1)
        def _():
            fold_y2(step // 2)
            fold_y1(2 + step // 2)

        return carry

    lax.fori_loop(0, STEPS, forward_step, 0)
    lax.fori_loop(0, STEPS, rims_step, 0)
    lax.fori_loop(0, STEPS, own_step, 0)
    for step in (2, 3):
        fold_y2(step)

    rim_left = remote(back_rim.at[0], back_in.at[0:SENT], back_s.at[0], back_r.at[0], left)
    rim_right = remote(back_rim.at[1], back_in.at[SENT : 2 * SENT], back_s.at[1], back_r.at[1], right)
    rim_left.wait_recv()
    rim_right.wait_recv()
    for number in range(4):
        remote(
            back_four.at[number], back_four_in.at[number], bfour_s.at[number], bfour_r.at[number], fours[number]
        ).wait_recv()
    for part, out in ((0, dk_ref), (1, dv_ref)):
        for column in range(0, WIDTH, 256):
            columns = slice(column, column + 256)
            rows4 = [back_four_in[number, :, columns].astype(F32)[8 * part : 8 * part + 8] for number in range(4)]
            back[part, 96:128, columns] = jnp.concatenate(rows4, axis=0).astype(BF16)
            total = own[part, :, columns] + dot_nn(spread[...], back[part, :, columns])
            out[:, columns] = (total + dot_nn(spread_back[part], back_in[:, columns])).astype(BF16)

    all_z = remote(z_in, z_in, z_s.at[0], z_r.at[0], right)
    all_z.wait_recv()
    mine = kept[STEPS - 1, pl.ds(pl.multiple_of(odd_z * PAIR + x * 32, 32), 32), :]
    gw_ref[...] = (mine + jnp.sum(z_in[...].astype(F32), axis=0)) * FACTOR

    sent_rims = [
        remote(rim.at[side], rim_in.at[side], rim_s.at[side], rim_r.at[0], right) for side in (0, 1)
    ]
    sent_four = [
        remote(four, four_in.at[number], four_s.at[number], four_r.at[number], fours[number]) for number in range(4)
    ]
    for copy in sent_rims + sent_four + twin_columns + [rim_left, rim_right, all_z]:
        copy.wait_send()
    for number in range(4):
        remote(
            back_four.at[number], back_four_in.at[number], bfour_s.at[number], bfour_r.at[number], fours[number]
        ).wait_send()

    def wait_sends(step, carry):
        copy_a(step).wait_send()
        for copy in copies_y1(step) + copies_y2(step):
            copy.wait_send()
        return carry

    lax.fori_loop(0, STEPS, wait_sends, 0)


def hand_on(*refs):
    given, results, sems = refs[0:4], refs[4:8], refs[8]
    stores = [pltpu.make_async_copy(given[i], results[i], sems.at[i]) for i in range(4)]
    for store in stores:
        store.start()
    for store in stores:
        store.wait()


def on_device(queries, keys, values, d_out, w_out):
    dma = pltpu.SemaphoreType.DMA
    any_space = pl.BlockSpec(memory_space=pl.ANY)
    rows_shape = jax.ShapeDtypeStruct((ROWS, WIDTH), BF16)
    grad_shape = jax.ShapeDtypeStruct((32, 128), F32)
    results = (rows_shape, rows_shape, rows_shape, grad_shape)
    held = tuple(pltpu.VMEM(result.shape, result.dtype) for result in results)
    vmem = pl.BlockSpec(memory_space=pltpu.VMEM)
    outs = pl.pallas_call(
        kernel,
        out_shape=held,
        in_specs=[any_space] * 5,
        out_specs=(vmem,) * 4,
        scratch_shapes=[
            pltpu.VMEM((ROWS, WIDTH), BF16),
            pltpu.VMEM((ROWS, WIDTH), BF16),
            pltpu.VMEM((WIDTH, WIDTH), BF16),
            pltpu.VMEM((ROWS, WIDTH), BF16),
            pltpu.VMEM((2, KEYS, WIDTH), BF16),
            pltpu.VMEM((KEYS, 2 * ROWS), F32),
            pltpu.VMEM((ROWS, ROWS), BF16),
            pltpu.VMEM((2, ROWS, 2 * SENT), BF16),
            pltpu.VMEM((2, ROWS, SENT), BF16),
            pltpu.VMEM((2, SENT, ROWS), BF16),
            pltpu.VMEM((2, SENT, WIDTH), BF16),
            pltpu.VMEM((2, SENT, WIDTH), BF16),
            pltpu.VMEM((16, WIDTH), BF16),
            pltpu.VMEM((4, 16, WIDTH), BF16),
            pltpu.VMEM((PAIRS, KEYS, 2 * ROWS), F32),
            pltpu.VMEM((PAIRS, KEYS, 2 * ROWS), BF16),
            pltpu.VMEM((PAIRS, KEYS, 2 * ROWS), BF16),
            pltpu.VMEM((2, ROWS, WIDTH), F32),
            pltpu.VMEM((2, ROWS, WIDTH), BF16),
            pltpu.VMEM((2 * SENT, WIDTH), BF16),
            pltpu.VMEM((2, SENT, WIDTH), BF16),
            pltpu.VMEM((4, 16, WIDTH), BF16),
            pltpu.VMEM((4, 16, WIDTH), BF16),
            pltpu.VMEM((STEPS, WIDE, 2 * ROWS), BF16),
            pltpu.VMEM((2 * ROWS, 512), BF16),
            pltpu.VMEM((STEPS, WIDE, 128), F32),
            pltpu.VMEM((STEPS, WIDE, 128), F32),
            pltpu.VMEM((STEPS, 2, WIDE, 128), BF16),
            pltpu.VMEM((STEPS, 2, WIDE, 128), BF16),
            pltpu.VMEM((STEPS, 2, 128, 128), BF16),
            pltpu.VMEM((STEPS, 2, 128, 128), BF16),
            pltpu.VMEM((STEPS, WIDE, 128), BF16),
            pltpu.VMEM((N_SEQ - 1, 32, 128), BF16),
            dma((5,)),
            dma((2,)), dma((2 * STEPS,)),
            dma((4,)), dma((4 * STEPS,)),
            dma((4,)), dma((4,)),
            dma((STEPS,)), dma((STEPS,)),
            dma((2 * STEPS,)), dma((2 * STEPS,)),
            dma((2 * STEPS,)), dma((2 * STEPS,)),
            dma((1,)), dma((1,)),
            dma((2,)), dma((2,)),
            dma((4,)), dma((4,)),
        ],
        compiler_params=pltpu.CompilerParams(
            collective_id=0, has_side_effects=True, vmem_limit_bytes=VMEM_BYTES
        ),
    )(queries[0], keys[0], values[0], d_out[0], w_out)
    d_queries, d_keys, d_values, grad_w = pl.pallas_call(
        hand_on,
        out_shape=results,
        in_specs=[any_space] * 4,
        out_specs=(any_space,) * 4,
        scratch_shapes=[dma((4,))],
        compiler_params=pltpu.CompilerParams(vmem_limit_bytes=4 * 1024 * 1024),
    )(*outs)
    return d_queries[None], d_keys[None], d_values[None], grad_w


def solution(mesh):
    placed = P("dp", "seq", None)
    return jax.shard_map(
        on_device,
        mesh=mesh,
        in_specs=(placed, placed, placed, placed, P()),
        out_specs=(placed, placed, placed, P("seq", "dp")),
        check_vma=False,
    )
```

```python
import jax
import jax.numpy as jnp
from jax import lax
from jax.experimental import pallas as pl
from jax.experimental.pallas import tpu as pltpu
from jax.sharding import PartitionSpec as P

ROWS = 128
WIDTH = 1024
PAIR = 128
PAIRS = 8
KEYS = 384
N_SEQ = 32
X, Z = 4, 8
FACTOR = 32768 ** (-0.5)
STEPS = 4
SENT = 80
WIDE = 256
VMEM_BYTES = 56 * 1024 * 1024
MESH = pl.DeviceIdType.MESH
F32 = jnp.float32
BF16 = jnp.bfloat16

OWN1, OWN2, LEFT, RIGHT, LEFT4, RIGHT4 = 128, 192, 224, 288, 352, 368


def dot_nt(a, b):
    return lax.dot_general(a, b, (((1,), (1,)), ((), ())), preferred_element_type=F32)


def dot_tn(a, b):
    return lax.dot_general(a, b, (((0,), (0,)), ((), ())), preferred_element_type=F32)


def dot_nn(a, b):
    return lax.dot_general(a, b, (((1,), (0,)), ((), ())), preferred_element_type=F32)


def two_heads(block, scale):
    lane = lax.broadcasted_iota(jnp.int32, (1, PAIR), 1)
    first = jnp.where(lane < 64, scale, 0.0).astype(BF16)
    second = jnp.where(lane < 64, 0.0, scale).astype(BF16)
    return jnp.concatenate([block * first, block * second], axis=0)


def one_of_two(both):
    row = lax.broadcasted_iota(jnp.int32, (PAIR, ROWS), 0)
    return jnp.where(row < 64, both[:, :ROWS], both[:, ROWS:])


def pool_matrix():
    row = lax.broadcasted_iota(jnp.int32, (ROWS, ROWS), 0)
    token = lax.broadcasted_iota(jnp.int32, (ROWS, ROWS), 1)
    level = jnp.where(row < 64, 1, jnp.where(row < 96, 2, jnp.where(row < 112, 3, 4)))
    base = jnp.where(row < 64, 0, jnp.where(row < 96, 64, jnp.where(row < 112, 96, 112)))
    matrix = jnp.where(lax.shift_right_logical(token, level) == row - base, 1.0, 0.0).astype(BF16)
    row = lax.broadcasted_iota(jnp.int32, (ROWS, 1), 0)
    scale = jnp.where(
        row < 64, 2.0 ** (-0.5), jnp.where(row < 96, 0.5, jnp.where(row < 112, 2.0 ** (-1.5), 0.25))
    ).astype(F32)
    return matrix, scale


def rim_row(row, side):
    level = lax.rem(row, 64) // 16
    within = lax.rem(row, 16)
    if side == 0:
        within = within + jnp.where(level == 0, 112, jnp.where(level == 1, 48, jnp.where(level == 2, 16, 0)))
    return row // 64, level, within


def sent_row(row, side):
    fine = row < 32
    level = jnp.where(fine, 0, (row - 16) // 16)
    part = jnp.where(fine, row // 16, lax.rem(row, 16) // 8)
    within = jnp.where(fine, lax.rem(row, 16), lax.rem(row, 8))
    if side == 0:
        base = jnp.where(fine, 112, jnp.where(level == 1, 48, jnp.where(level == 2, 16, 0)))
    else:
        base = jnp.where(fine, 0, 8)
    return part, level, lax.shift_left(base + within, level)


def rim_matrix(shape, rim_axis, side):
    part, level, position = rim_row(lax.broadcasted_iota(jnp.int32, shape, rim_axis), side)
    from_part, _, first = sent_row(lax.broadcasted_iota(jnp.int32, shape, 1 - rim_axis), side)
    covered = (part == from_part) & (lax.shift_right_logical(first, level) == position)
    return jnp.where(covered, 1.0, 0.0).astype(BF16)


def level_scale(level):
    return jnp.where(
        level == 0, 1.0, jnp.where(level == 1, 2.0 ** (-0.5), jnp.where(level == 2, 0.5, 2.0 ** (-1.5)))
    ).astype(F32)


def rim_scale(side):
    _, level, position = rim_row(lax.broadcasted_iota(jnp.int32, (ROWS, 1), 0), side)
    token = lax.shift_left(position, level)
    if side == 0:
        source = jnp.where(token >= 112, 0, jnp.where(token >= 96, 1, jnp.where(token >= 64, 2, 3)))
    else:
        source = jnp.where(token < 16, 0, jnp.where(token < 32, 1, jnp.where(token < 64, 2, 3)))
    return level_scale(level - source)


def spread_matrix():
    token = lax.broadcasted_iota(jnp.int32, (ROWS, ROWS), 0)
    row = lax.broadcasted_iota(jnp.int32, (ROWS, ROWS), 1)
    level = jnp.where(row < 64, 1, jnp.where(row < 96, 2, 4))
    target = jnp.where(row < 64, row, jnp.where(row < 96, row - 64, lax.rem(row - 96, 8)))
    return jnp.where(lax.shift_right_logical(token, level) == target, 1.0, 0.0).astype(BF16)


def spread_sent(part):
    columns = []
    for side in (0, 1):
        token = lax.broadcasted_iota(jnp.int32, (ROWS, SENT), 0)
        of_part, level, first = sent_row(lax.broadcasted_iota(jnp.int32, (ROWS, SENT), 1), side)
        same = lax.shift_right_logical(token, level) == lax.shift_right_logical(first, level)
        columns.append(jnp.where((of_part == part) & same, 1.0, 0.0))
    return columns


def fill_bias(bias, device):
    token = lax.rem(lax.broadcasted_iota(jnp.int32, (16, 2 * ROWS), 1), ROWS)
    not_first = device > 0
    not_last = device < N_SEQ - 1

    def put(row, valid):
        bias[row : row + 16, :] = jnp.where(valid, 0.0, -1e30).astype(F32)

    for block in range(8):
        near = token // 16 - block
        put(16 * block, (near >= -1) & (near <= 1))
    for block in range(4):
        near = token // 32 - block
        put(OWN1 + 16 * block, (near == -1) | (near == 1))
    for block in range(2):
        put(OWN2 + 16 * block, token // 64 != block)
    for level in range(4):
        span = 16 * 2**level
        put(LEFT + 16 * level, (token < span) & not_first)
        put(RIGHT + 16 * level, (token >= ROWS - span) & not_last)
    always = token >= 0
    put(LEFT4, always & (device >= 2))
    put(RIGHT4, always & (device < N_SEQ - 2))


def kernel(
    q_hbm, k_hbm, v_hbm, d_hbm, w_hbm,
    dq_ref, dk_ref, dv_ref, gw_ref, q, d, w, g, kv, bias, spread, spread_back, unfold, fold, scale_in, scale_out,
    rim, rim_in, four, four_in,
    weights, weights_half, grad_scores, own, back, back_in, back_rim, back_four, back_four_in,
    pairs_a, pairs_d, kept, kept2, y1_out, y1_in, y2_out, y2_in, z_out, z_in,
    in_sem, rim_s, rim_r, four_s, four_r, d2_s, d2_r, a_s, a_r, y1_s, y1_r, y2_s, y2_r,
    z_s, z_r, back_s, back_r, bfour_s, bfour_r,
):
    seq = lax.axis_index("seq")
    dp = lax.axis_index("dp")
    z, x = lax.div(seq, X), lax.rem(seq, X)
    y, core = lax.div(dp, 2), lax.rem(dp, 2)
    ya = y + 1 - 2 * lax.rem(y, 2)
    yb = 3 - y
    yo = 3 - ya
    pair_of = lax.div(seq, 2)
    parity = lax.rem(seq, 2)

    def at(seq_to, dp_to):
        return {"seq": seq_to, "dp": dp_to}

    right = at(lax.rem(seq + 1, N_SEQ), dp)
    left = at(lax.rem(seq + N_SEQ - 1, N_SEQ), dp)
    twin = at(seq, 2 * y + 1 - core)
    at_ya = at(seq, 2 * ya + core)
    at_yb = at(seq, 2 * yb + core)
    fours = []
    for side in (0, 1):
        block = lax.rem(pair_of + (N_SEQ // 2 - 1 if side == 0 else 1), N_SEQ // 2)
        for part in (0, 1):
            fours.append(at(2 * block + part, dp))

    def remote(src, dst, send, recv, device_id):
        return pltpu.make_async_remote_copy(
            src_ref=src, dst_ref=dst, send_sem=send, recv_sem=recv, device_id=device_id, device_id_type=MESH
        )

    load_k = pltpu.make_async_copy(k_hbm, kv.at[0, 0:ROWS], in_sem.at[0])
    load_v = pltpu.make_async_copy(v_hbm, kv.at[1, 0:ROWS], in_sem.at[1])
    load_d = pltpu.make_async_copy(d_hbm, d, in_sem.at[2])
    load_w = pltpu.make_async_copy(w_hbm, w, in_sem.at[3])
    load_q = pltpu.make_async_copy(q_hbm, q, in_sem.at[4])
    for load in (load_k, load_v, load_d, load_w, load_q):
        load.start()
    barrier = pltpu.get_barrier_semaphore()
    partners = [right, left, twin, at_ya, at_yb] + fours
    for partner in partners:
        pl.semaphore_signal(barrier, inc=1, device_id=partner, device_id_type=MESH)

    def greet(number, carry):
        pl.semaphore_signal(barrier, inc=1, device_id=at(lax.rem(seq + number, N_SEQ), dp), device_id_type=MESH)
        return carry

    lax.fori_loop(1, N_SEQ, greet, 0)

    matrix, scale = pool_matrix()
    pooled = []
    for part, load in ((0, load_k), (1, load_v)):
        load.wait()
        sums = dot_nn(matrix, kv[part, 0:ROWS, :]) * scale
        kv[part, OWN1:LEFT, :] = sums[0:96].astype(BF16)
        rim[0, 16 * part : 16 * part + 16] = kv[part, 0:16, :]
        rim[1, 16 * part : 16 * part + 16] = kv[part, 112:128, :]
        pooled.append(sums)

    def of_both(row):
        return jnp.concatenate([sums[row : row + 8] for sums in pooled], axis=0).astype(BF16)

    for side, rows in ((0, (8, 72, 104)), (1, (48, 80, 96))):
        for number, row in enumerate(rows):
            rim[side, 32 + 16 * number : 48 + 16 * number] = of_both(row)
    four[...] = of_both(112)

    pl.semaphore_wait(barrier, len(partners) + N_SEQ - 1)

    def part_of(z_at, step):
        return lax.rem(lax.div(z_at, 2) + 2 - step + 3 * lax.div(step, 2) - 2 * lax.div(step, 3), STEPS)

    def lanes_at(z_at, step):
        return pl.ds(pl.multiple_of(part_of(z_at, step) * WIDE, WIDE), WIDE)

    def lanes_of(step):
        return lanes_at(z, step)

    def pair_lanes(step, pair):
        return pl.ds(pl.multiple_of(part_of(z, step) * WIDE + pair * PAIR, PAIR), PAIR)

    def rim_copies(step, lanes_to):
        copies = []
        for side, partner in ((0, left), (1, right)):
            lanes = lanes_to(partner, step)
            copies.append(
                remote(
                    rim.at[side, :, lanes],
                    rim_in.at[1 - side, :, lanes],
                    rim_s.at[side],
                    rim_r.at[side * STEPS + step],
                    partner,
                )
            )
        return copies

    def four_copies(step, lanes_to):
        copies = []
        for number, partner in enumerate(fours):
            slot = parity + (2 if number < 2 else 0)
            lanes = lanes_to(partner, step)
            copies.append(
                remote(
                    four.at[:, lanes],
                    four_in.at[slot, :, lanes],
                    four_s.at[number],
                    four_r.at[slot * STEPS + step],
                    partner,
                )
            )
        return copies

    for step in range(STEPS):
        for copies in (four_copies, rim_copies):
            for copy in copies(step, lambda partner, step: lanes_at(lax.div(partner["seq"], X), step)):
                copy.start()

    def wait_rims(step):
        lanes = lanes_of(step)
        for copy in rim_copies(step, lambda partner, step: lanes):
            copy.wait_recv()
        for side, row in ((0, LEFT), (1, RIGHT)):
            rows = dot_nn(unfold[side], rim_in[side, :, lanes]) * scale_in[side]
            kv[0, row : row + 64, lanes] = rows[0:64].astype(BF16)
            kv[1, row : row + 64, lanes] = rows[64:128].astype(BF16)
        for number in range(4):
            remote(
                four.at[:, lanes],
                four_in.at[number, :, lanes],
                four_s.at[number],
                four_r.at[number * STEPS + step],
                fours[number],
            ).wait_recv()
        for side, row in ((0, LEFT4), (1, RIGHT4)):
            one = four_in[2 * side, :, lanes].astype(F32)
            two = four_in[2 * side + 1, :, lanes].astype(F32)
            for part in (0, 1):
                kv[part, row : row + 16, lanes] = jnp.concatenate(
                    [one[8 * part : 8 * part + 8], two[8 * part : 8 * part + 8]], axis=0
                ).astype(BF16)

    load_d.wait()
    mine_rows = pl.ds(pl.multiple_of(core * ROWS, ROWS), ROWS)
    twin_columns = []
    for number, y_to in enumerate((y, ya, yb, yo)):
        columns = slice(number * PAIR, (number + 1) * PAIR)
        theirs = pl.ds(pl.multiple_of(y_to * 256 + (1 - core) * PAIR, PAIR), PAIR)
        copy = remote(
            d.at[:, theirs], pairs_d.at[mine_rows, columns], d2_s.at[number], d2_r.at[number], twin
        )
        copy.start()
        twin_columns.append(copy)

    fill_bias(bias, seq)
    scale_out[...] = level_scale(lax.rem(lax.broadcasted_iota(jnp.int32, (ROWS, PAIR), 0), 64) // 16)
    for side in (0, 1):
        scale_in[side] = jnp.broadcast_to(rim_scale(side), (ROWS, WIDE))
        unfold[side] = rim_matrix((ROWS, SENT), 0, side)
        fold[side] = rim_matrix((SENT, ROWS), 1, side)
    for number, y_to in enumerate((y, ya, yb, yo)):
        ours = pl.ds(pl.multiple_of(y_to * 256 + core * PAIR, PAIR), PAIR)
        pairs_d[mine_rows, number * PAIR : (number + 1) * PAIR] = d[:, ours]
    load_w.wait()
    for column in range(0, WIDTH, 256):
        g[:, column : column + 256] = dot_nt(d[...], w[column : column + 256, :]).astype(BF16)
    load_q.wait()

    for copy in twin_columns:
        copy.wait_recv()

    mine_lanes = pl.ds(pl.multiple_of(core * ROWS, ROWS), ROWS)

    def copy_a(step):
        block = pairs_a.at[step, :, mine_lanes]
        return remote(block, block, a_s.at[step], a_r.at[step], twin)

    def copies_y1(step):
        return (
            remote(y1_out.at[step, 0], y1_in.at[step, 0], y1_s.at[2 * step], y1_r.at[2 * step], at_ya),
            remote(y1_out.at[step, 1], y1_in.at[step, 1], y1_s.at[2 * step + 1], y1_r.at[2 * step + 1], at_yb),
        )

    def copies_y2(step):
        return (
            remote(y2_out.at[step, 0], y2_in.at[step, 0], y2_s.at[2 * step], y2_r.at[2 * step], at_yb),
            remote(y2_out.at[step, 1], y2_in.at[step, 1], y2_s.at[2 * step + 1], y2_r.at[2 * step + 1], at_ya),
        )

    odd_z = lax.rem(z, 2)

    def send_z(step, pair):
        z_to = 2 * part_of(z, step) + pair
        last = lax.div(step, STEPS - 1)
        same = last * (odd_z if pair else 1 - odd_z)

        def copy(apart):
            x_to = lax.rem(x + apart, X)
            rows = pl.ds(pl.multiple_of(pair * PAIR + x_to * 32, 32), 32)
            slot = 8 * step + (1 - last) * 4 * odd_z + 3 * same + apart
            return remote(
                z_out.at[step, rows], z_in.at[slot], z_s.at[0], z_r.at[0], at(z_to * X + x_to, dp)
            )

        @pl.when(same == 0)
        def _():
            copy(0).start()

        for apart in range(1, X):
            copy(apart).start()

    def forward(step):
        lanes = [pair_lanes(step, pair) for pair in (0, 1)]
        query_rows = [two_heads(q[:, at_lanes], 0.125) for at_lanes in lanes]
        scores = [dot_nt(kv[0, :, at_lanes], rows) + bias[...] for at_lanes, rows in zip(lanes, query_rows)]
        tops = [jnp.max(score, axis=0, keepdims=True) for score in scores]
        exponents = [jnp.exp(score - top) for score, top in zip(scores, tops)]
        shares = [1.0 / jnp.sum(exponent, axis=0, keepdims=True) for exponent in exponents]
        normal = [exponent * share for exponent, share in zip(exponents, shares)]
        halves = [weight.astype(BF16) for weight in normal]
        attended = [
            one_of_two(dot_tn(kv[1, :, at_lanes], half)).astype(BF16) for at_lanes, half in zip(lanes, halves)
        ]
        for pair in (0, 1):
            weights[2 * step + pair] = normal[pair]
            weights_half[2 * step + pair] = halves[pair]
            pairs_a[step, pair * PAIR : (pair + 1) * PAIR, mine_lanes] = attended[pair]
        copy_a(step).start()

    def project(step):
        copy_a(step).wait_recv()
        partial = dot_nn(pairs_a[step], pairs_d[...])
        kept[step] = partial[:, 0:128]
        kept2[step, 0:128] = partial[0:128, 256:384]
        kept2[step, 128:256] = partial[128:256, 128:256]
        y1_out[step, 0, 0:128] = partial[0:128, 128:256].astype(BF16)
        y1_out[step, 0, 128:256] = partial[0:128, 384:512].astype(BF16)
        y1_out[step, 1, 0:128] = partial[128:256, 256:384].astype(BF16)
        y1_out[step, 1, 128:256] = partial[128:256, 384:512].astype(BF16)
        for copy in copies_y1(step):
            copy.start()

    def fold_y1(step):
        for copy in copies_y1(step):
            copy.wait_recv()
        for half in (0, 1):
            rows = slice(128 * half, 128 * half + 128)
            kept[step, rows] = kept[step, rows] + y1_in[step, half, 0:128].astype(F32)
            y2_out[step, half] = (kept2[step, rows] + y1_in[step, half, 128:256].astype(F32)).astype(BF16)
        for copy in copies_y2(step):
            copy.start()

    def fold_y2(step):
        for copy in copies_y2(step):
            copy.wait_recv()
        for half in (0, 1):
            rows = slice(128 * half, 128 * half + 128)
            total = kept[step, rows] + y2_in[step, half].astype(F32)
            kept[step, rows] = total
            z_out[step, rows] = total.astype(BF16)
        for pair in (0, 1):
            send_z(step, pair)

    def backward_rims(step):
        steps = (2 * step, 2 * step + 1)
        lanes = [pair_lanes(step, pair) for pair in (0, 1)]
        query_rows = [two_heads(q[:, at_lanes], 0.125) for at_lanes in lanes]
        grad_rows = [two_heads(g[:, at_lanes], 1.0) for at_lanes in lanes]
        d_probs = [dot_nt(kv[1, :, at_lanes], rows) for at_lanes, rows in zip(lanes, grad_rows)]
        normal = [weights[number] for number in steps]
        deltas = [jnp.sum(weight * d_prob, axis=0, keepdims=True) for weight, d_prob in zip(normal, d_probs)]
        d_scores = [
            (weight * (d_prob - delta)).astype(BF16) for weight, d_prob, delta in zip(normal, d_probs, deltas)
        ]
        d_keys = [dot_nn(d_score[LEFT:], rows) for d_score, rows in zip(d_scores, query_rows)]
        d_values = [dot_nn(weights_half[number, LEFT:, :], rows) for number, rows in zip(steps, grad_rows)]
        for number, at_lanes, d_score, d_key, d_value in zip(steps, lanes, d_scores, d_keys, d_values):
            grad_scores[number] = d_score
            for side in (0, 1):
                rows = slice(64 * side, 64 * side + 64)
                grads = jnp.concatenate([d_key[rows], d_value[rows]], axis=0) * scale_out[...]
                back_rim[side, :, at_lanes] = dot_nn(fold[side], grads.astype(BF16)).astype(BF16)
            for number in range(4):
                rows = slice(128 + 8 * number, 136 + 8 * number)
                both = jnp.concatenate([d_key[rows], d_value[rows]], axis=0) * 0.25
                back_four[number, :, at_lanes] = both.astype(BF16)
        for at_lanes in [lanes_of(step)]:
            remote(
                back_rim.at[0, :, at_lanes], back_in.at[0:SENT, at_lanes], back_s.at[0], back_r.at[0], left
            ).start()
            remote(
                back_rim.at[1, :, at_lanes], back_in.at[SENT : 2 * SENT, at_lanes], back_s.at[1], back_r.at[1], right
            ).start()
            for number, partner in enumerate(fours):
                slot = parity + (2 if number < 2 else 0)
                remote(
                    back_four.at[number, :, at_lanes],
                    back_four_in.at[slot, :, at_lanes],
                    bfour_s.at[number],
                    bfour_r.at[slot],
                    partner,
                ).start()

    def backward_own(step):
        steps = (2 * step, 2 * step + 1)
        lanes = [pair_lanes(step, pair) for pair in (0, 1)]
        query_rows = [two_heads(q[:, at_lanes], 0.125) for at_lanes in lanes]
        grad_rows = [two_heads(g[:, at_lanes], 1.0) for at_lanes in lanes]
        d_queries = [
            one_of_two(dot_tn(kv[0, :, at_lanes], grad_scores[number])) * 0.125 for number, at_lanes in zip(steps, lanes)
        ]
        d_keys = [dot_nn(grad_scores[number, 0:LEFT, :], rows) for number, rows in zip(steps, query_rows)]
        d_values = [dot_nn(weights_half[number, 0:LEFT, :], rows) for number, rows in zip(steps, grad_rows)]
        for at_lanes, d_query, d_key, d_value in zip(lanes, d_queries, d_keys, d_values):
            dq_ref[:, at_lanes] = d_query.T.astype(BF16)
            for part, grad in ((0, d_key), (1, d_value)):
                own[part, :, at_lanes] = grad[0:ROWS]
                back[part, 0:64, at_lanes] = (grad[OWN1:OWN2] * 2.0 ** (-0.5)).astype(BF16)
                back[part, 64:96, at_lanes] = (grad[OWN2:LEFT] * 0.5).astype(BF16)

    def forward_step(step, carry):
        wait_rims(step)
        forward(step)

        @pl.when(step >= 1)
        def _():
            project(step - 1)

        return carry

    def rims_step(step, carry):
        backward_rims(step)

        @pl.when(step == 0)
        def _():
            project(step + 3)

        @pl.when(lax.rem(step, 2) == 1)
        def _():
            fold_y1(step // 2)

        return carry

    def own_step(step, carry):
        backward_own(step)

        @pl.when(lax.rem(step, 2) == 1)
        def _():
            fold_y2(step // 2)
            fold_y1(2 + step // 2)

        return carry

    lax.fori_loop(0, STEPS, forward_step, 0)
    lax.fori_loop(0, STEPS, rims_step, 0)
    lax.fori_loop(0, STEPS, own_step, 0)
    for step in (2, 3):
        fold_y2(step)

    spread[...] = spread_matrix()
    for part in (0, 1):
        spread_back[part] = jnp.concatenate(spread_sent(part), axis=1).astype(BF16)
    rim_left = remote(back_rim.at[0], back_in.at[0:SENT], back_s.at[0], back_r.at[0], left)
    rim_right = remote(back_rim.at[1], back_in.at[SENT : 2 * SENT], back_s.at[1], back_r.at[1], right)
    rim_left.wait_recv()
    rim_right.wait_recv()
    for number in range(4):
        remote(
            back_four.at[number], back_four_in.at[number], bfour_s.at[number], bfour_r.at[number], fours[number]
        ).wait_recv()
    for part, out in ((0, dk_ref), (1, dv_ref)):
        for column in range(0, WIDTH, 256):
            columns = slice(column, column + 256)
            rows4 = [back_four_in[number, :, columns].astype(F32)[8 * part : 8 * part + 8] for number in range(4)]
            back[part, 96:128, columns] = jnp.concatenate(rows4, axis=0).astype(BF16)
            total = own[part, :, columns] + dot_nn(spread[...], back[part, :, columns])
            out[:, columns] = (total + dot_nn(spread_back[part], back_in[:, columns])).astype(BF16)

    all_z = remote(z_in, z_in, z_s.at[0], z_r.at[0], right)
    all_z.wait_recv()
    mine = kept[STEPS - 1, pl.ds(pl.multiple_of(odd_z * PAIR + x * 32, 32), 32), :]
    gw_ref[...] = (mine + jnp.sum(z_in[...].astype(F32), axis=0)) * FACTOR

    sent_rims = [
        remote(rim.at[side], rim_in.at[side], rim_s.at[side], rim_r.at[0], right) for side in (0, 1)
    ]
    sent_four = [
        remote(four, four_in.at[number], four_s.at[number], four_r.at[number], fours[number]) for number in range(4)
    ]
    for copy in sent_rims + sent_four + twin_columns + [rim_left, rim_right, all_z]:
        copy.wait_send()
    for number in range(4):
        remote(
            back_four.at[number], back_four_in.at[number], bfour_s.at[number], bfour_r.at[number], fours[number]
        ).wait_send()

    def wait_sends(step, carry):
        copy_a(step).wait_send()
        for copy in copies_y1(step) + copies_y2(step):
            copy.wait_send()
        return carry

    lax.fori_loop(0, STEPS, wait_sends, 0)


def hand_on(*refs):
    given, results, sems = refs[0:4], refs[4:8], refs[8]
    stores = [pltpu.make_async_copy(given[i], results[i], sems.at[i]) for i in range(4)]
    for store in stores:
        store.start()
    for store in stores:
        store.wait()


def on_device(queries, keys, values, d_out, w_out):
    dma = pltpu.SemaphoreType.DMA
    any_space = pl.BlockSpec(memory_space=pl.ANY)
    rows_shape = jax.ShapeDtypeStruct((ROWS, WIDTH), BF16)
    grad_shape = jax.ShapeDtypeStruct((32, 128), F32)
    results = (rows_shape, rows_shape, rows_shape, grad_shape)
    held = tuple(pltpu.VMEM(result.shape, result.dtype) for result in results)
    vmem = pl.BlockSpec(memory_space=pltpu.VMEM)
    outs = pl.pallas_call(
        kernel,
        out_shape=held,
        in_specs=[any_space] * 5,
        out_specs=(vmem,) * 4,
        scratch_shapes=[
            pltpu.VMEM((ROWS, WIDTH), BF16),
            pltpu.VMEM((ROWS, WIDTH), BF16),
            pltpu.VMEM((WIDTH, WIDTH), BF16),
            pltpu.VMEM((ROWS, WIDTH), BF16),
            pltpu.VMEM((2, KEYS, WIDTH), BF16),
            pltpu.VMEM((KEYS, 2 * ROWS), F32),
            pltpu.VMEM((ROWS, ROWS), BF16),
            pltpu.VMEM((2, ROWS, 2 * SENT), BF16),
            pltpu.VMEM((2, ROWS, SENT), BF16),
            pltpu.VMEM((2, SENT, ROWS), BF16),
            pltpu.VMEM((2, ROWS, WIDE), F32),
            pltpu.VMEM((ROWS, PAIR), F32),
            pltpu.VMEM((2, SENT, WIDTH), BF16),
            pltpu.VMEM((2, SENT, WIDTH), BF16),
            pltpu.VMEM((16, WIDTH), BF16),
            pltpu.VMEM((4, 16, WIDTH), BF16),
            pltpu.VMEM((PAIRS, KEYS, 2 * ROWS), F32),
            pltpu.VMEM((PAIRS, KEYS, 2 * ROWS), BF16),
            pltpu.VMEM((PAIRS, KEYS, 2 * ROWS), BF16),
            pltpu.VMEM((2, ROWS, WIDTH), F32),
            pltpu.VMEM((2, ROWS, WIDTH), BF16),
            pltpu.VMEM((2 * SENT, WIDTH), BF16),
            pltpu.VMEM((2, SENT, WIDTH), BF16),
            pltpu.VMEM((4, 16, WIDTH), BF16),
            pltpu.VMEM((4, 16, WIDTH), BF16),
            pltpu.VMEM((STEPS, WIDE, 2 * ROWS), BF16),
            pltpu.VMEM((2 * ROWS, 512), BF16),
            pltpu.VMEM((STEPS, WIDE, 128), F32),
            pltpu.VMEM((STEPS, WIDE, 128), F32),
            pltpu.VMEM((STEPS, 2, WIDE, 128), BF16),
            pltpu.VMEM((STEPS, 2, WIDE, 128), BF16),
            pltpu.VMEM((STEPS, 2, 128, 128), BF16),
            pltpu.VMEM((STEPS, 2, 128, 128), BF16),
            pltpu.VMEM((STEPS, WIDE, 128), BF16),
            pltpu.VMEM((N_SEQ - 1, 32, 128), BF16),
            dma((5,)),
            dma((2,)), dma((2 * STEPS,)),
            dma((4,)), dma((4 * STEPS,)),
            dma((4,)), dma((4,)),
            dma((STEPS,)), dma((STEPS,)),
            dma((2 * STEPS,)), dma((2 * STEPS,)),
            dma((2 * STEPS,)), dma((2 * STEPS,)),
            dma((1,)), dma((1,)),
            dma((2,)), dma((2,)),
            dma((4,)), dma((4,)),
        ],
        compiler_params=pltpu.CompilerParams(
            collective_id=0, has_side_effects=True, vmem_limit_bytes=VMEM_BYTES
        ),
    )(queries[0], keys[0], values[0], d_out[0], w_out)
    d_queries, d_keys, d_values, grad_w = pl.pallas_call(
        hand_on,
        out_shape=results,
        in_specs=[any_space] * 4,
        out_specs=(any_space,) * 4,
        scratch_shapes=[dma((4,))],
        compiler_params=pltpu.CompilerParams(vmem_limit_bytes=4 * 1024 * 1024),
    )(*outs)
    return d_queries[None], d_keys[None], d_values[None], grad_w


def solution(mesh):
    placed = P("dp", "seq", None)
    return jax.shard_map(
        on_device,
        mesh=mesh,
        in_specs=(placed, placed, placed, placed, P()),
        out_specs=(placed, placed, placed, P("seq", "dp")),
        check_vma=False,
    )
```
